128 devices in a mesh: segment: 2 (over core), mp: 4 (over x), dp: 16 (over z, y).
Axes of the slice: x: 4, y: 4, z: 4, core: 2. Of those that a mesh axis runs over, the one named last changes fastest.
Arguments:
- patches: bfloat16 [128, 32, 2560], P(('segment', 'dp')), may hold values from -6 to 6
- merger_weight: bfloat16 [2560, 4096], P(None, 'mp'), may hold values from -0.125 to 0.125
- image_counts: int32 [128], replicated, may hold values from 1 to 32, as said below
- routing: int32 [128], replicated, may hold values from 0 to 127, as said below
- text_embed: bfloat16 [2, 2048, 4096], P(None, 'dp', 'mp'), may hold values from -6 to 6
- llm_weight: bfloat16 [2, 4096, 4096], P('segment', None, 'mp'), may hold values from -0.046875 to 0.046875
- upstream: bfloat16 [2, 2048, 4096], P(None, 'dp', 'mp'), may hold values from -0.4375 to 0.4375
Outputs:
- llm_grad: float32 [2, 4096, 4096], P('segment', 'dp', 'mp')
- merger_grad: float32 [2560, 4096], P(('segment', 'dp'), 'mp')
The draws below stay inside these ranges and needn't reach their ends.
Inputs may be any that keep to these rules, and one draw needn't show every extreme that they name: Sample k has image_counts[k] image rows; one sample of every draw has all 32. `routing`: each slot is named by exactly one sample; the 4 samples k that share k // 4 name slots of 4 different replicas.
All inputs are finite; a program needn't handle non-finite values.
Results may differ from the reference program's by a relative error of at most 0.022.
Values may be sent and summed in bfloat16 or wider, within the bound.
No kernel may reach another device: no remote copies, remote signals or barrier semaphores. Data moves between devices by JAX's collectives and lax.ppermute only.
A program may use at most 192 MiB of HBM per device.

```python
import jax
import jax.numpy as jnp
from jax import lax

FEATURES = 4096
MERGER = 2560
SLOT_ROWS = 32
MICRO = 2
SAMPLES_MB = 4
TOKENS_MB = 128
SECTIONS = 2
ENCODE_DEV = 4
SAMPLES = 128
ALL_ROWS = 2048
N_SEGMENT = 2
N_MP = 4
N_DP = 16


def draw_image_counts(key, part):
    key = jax.random.fold_in(key, 11)
    first_key, second_key = jax.random.split(key)
    counts = jax.random.randint(first_key, (SAMPLES,), 1, 2 * SLOT_ROWS // 3 + 1)
    chosen = jax.random.randint(second_key, (), 0, SAMPLES)
    return jnp.where(jnp.arange(SAMPLES) == chosen, SLOT_ROWS, counts).astype(jnp.int32)


def draw_routing(key, part):
    key = jax.random.fold_in(key, 23)
    table_key, group_key, offset_key, score_key = jax.random.split(key, 4)
    replica_table = jax.random.permutation(table_key, N_DP).astype(jnp.int32)
    group_order = jax.random.permutation(group_key, N_SEGMENT * N_DP).astype(jnp.int32)
    offsets = jax.random.permutation(offset_key, N_DP).astype(jnp.int32)
    sample = jnp.arange(SAMPLES, dtype=jnp.int32)
    group = sample // ENCODE_DEV
    within = sample % ENCODE_DEV
    owner = replica_table[(group_order[group] + offsets[within]) % N_DP]
    scores = jax.random.permutation(score_key, SAMPLES).astype(jnp.int32)
    same = owner[:, None] == owner[None, :]
    lower = scores[None, :] < scores[:, None]
    rank = jnp.sum((same & lower).astype(jnp.int32), axis=1)
    return (owner * (SAMPLES // N_DP) + rank).astype(jnp.int32)


def levels(key, extent, cuts, smallest, largest):
    def one(dim, blocks):
        steps = jax.random.uniform(jax.random.fold_in(jax.random.fold_in(key, 6), dim), (blocks,), jnp.float32, smallest / len(cuts), largest / len(cuts))
        return jnp.repeat(jnp.exp(steps), extent[dim] // blocks).reshape((-1,) + (1,) * (len(extent) - dim - 1))

    level = one(*cuts[0])
    for cut in cuts[1:]:
        level = level * one(*cut)
    return level


def centred(rng, extent, spread, bound, cuts=(), kind=jnp.bfloat16):
    values = spread * jax.random.normal(rng, extent, jnp.float32)
    if cuts:
        values = values * levels(rng, extent, cuts, -0.22, 0.18)
    return jnp.clip(values, -bound, bound).astype(kind)


def setup_inputs(seed: int = 0) -> dict:
    streams_of = jax.random.split(jax.random.key(seed), 8)
    return {
        "patches": centred(streams_of[0], (SAMPLES, SLOT_ROWS, MERGER), 1.0, 6.0, ((0, 32),)),
        "merger_weight": centred(streams_of[1], (MERGER, FEATURES), MERGER ** -0.5, 0.125, ((1, 4),)),
        "image_counts": draw_image_counts(jax.random.fold_in(streams_of[7], 71), 0),
        "routing": draw_routing(jax.random.fold_in(streams_of[7], 71), 0),
        "text_embed": centred(streams_of[4], (MICRO, ALL_ROWS, FEATURES), 1.0, 6.0, ((1, 16), (2, 4))),
        "llm_weight": centred(streams_of[5], (SECTIONS, FEATURES, FEATURES), (4 * FEATURES) ** -0.5, 0.046875, ((0, 2), (2, 4))),
        "upstream": centred(streams_of[6], (MICRO, ALL_ROWS, FEATURES), 0.03, 0.4375, ((1, 16), (2, 4))),
    }


def gelu_back(preact, cotangent):
    _, pullback = jax.vjp(jax.nn.gelu, preact)
    return pullback(cotangent)[0]

def rounded_sum(running, product):
    return running + lax.optimization_barrier(product.astype(jnp.bfloat16)).astype(jnp.float32)

def input_grad(local_grad, weight):
    block_width = weight.shape[1] // N_MP
    running = jnp.zeros((local_grad.shape[0], weight.shape[0]), jnp.float32)
    for block_index in range(N_MP):
        offset = block_index * block_width
        product = jnp.dot(local_grad[:, offset:offset + block_width], weight[:, offset:offset + block_width].T, preferred_element_type=jnp.float32)
        running = rounded_sum(running, product)
    return running

def reference(patches, merger_weight, image_counts, routing, text_embed, llm_weight, upstream):
    activated = jax.nn.gelu(patches.astype(jnp.float32)).astype(jnp.bfloat16)
    flat_act = activated.reshape(SAMPLES * SLOT_ROWS, MERGER)
    embeds = jnp.dot(flat_act, merger_weight, preferred_element_type=jnp.float32).astype(jnp.bfloat16)
    embeds = embeds.reshape(SAMPLES, SLOT_ROWS, FEATURES)
    slot_owner = jnp.argsort(routing).astype(jnp.int32)
    position = jnp.arange(SLOT_ROWS)
    slot_mask = position[None, :] < image_counts[slot_owner][:, None]
    text_slots = text_embed.reshape(MICRO, N_DP, SAMPLES_MB, SLOT_ROWS, FEATURES).transpose(1, 0, 2, 3, 4).reshape(SAMPLES, SLOT_ROWS, FEATURES)
    start_rows = jnp.where(slot_mask[:, :, None], embeds[slot_owner], text_slots).reshape(N_DP, MICRO * TOKENS_MB, FEATURES)
    top_grads = upstream.reshape(MICRO, N_DP, TOKENS_MB, FEATURES).transpose(1, 0, 2, 3).reshape(N_DP, MICRO * TOKENS_MB, FEATURES)
    llm_grad = jnp.zeros((SECTIONS, FEATURES, FEATURES), jnp.float32)
    start_grads = []
    for replica in range(N_DP):
        hidden_rows = start_rows[replica]
        saved_rows = []
        saved_pre = []
        for section in range(SECTIONS):
            preact = jnp.dot(hidden_rows, llm_weight[section], preferred_element_type=jnp.float32)
            saved_rows.append(hidden_rows)
            saved_pre.append(preact)
            hidden_rows = (hidden_rows.astype(jnp.float32) + jax.nn.gelu(preact)).astype(jnp.bfloat16)
        cotangent = top_grads[replica]
        for section in reversed(range(SECTIONS)):
            local_grad = gelu_back(saved_pre[section], cotangent.astype(jnp.float32)).astype(jnp.bfloat16)
            product = jnp.dot(saved_rows[section].T, local_grad, preferred_element_type=jnp.float32)
            llm_grad = llm_grad.at[section].set(rounded_sum(llm_grad[section], product))
            inner_grad = input_grad(local_grad, llm_weight[section])
            cotangent = (cotangent.astype(jnp.float32) + inner_grad).astype(jnp.bfloat16)
        start_grads.append(cotangent)
    slot_grads = jnp.stack(start_grads).reshape(SAMPLES, SLOT_ROWS, FEATURES)
    sample_mask = position[None, :] < image_counts[:, None]
    image_grad = jnp.where(sample_mask[:, :, None], slot_grads[routing], jnp.zeros((), jnp.bfloat16))
    merger_grad = jnp.dot(flat_act.T, image_grad.reshape(SAMPLES * SLOT_ROWS, FEATURES), preferred_element_type=jnp.float32)
    return (llm_grad, merger_grad)
```

```python
import jax
import jax.numpy as jnp
from jax import lax
from jax.experimental import pallas as pl
from jax.experimental.pallas import tpu as pltpu
from jax.sharding import PartitionSpec as P

BF = jnp.bfloat16
F32 = jnp.float32
SIDE = 4
SLOTS = 8
ROWS = 32
MINE = 4
ANY = pl.BlockSpec(memory_space=pl.ANY)


def dot(a, b):
    return jnp.dot(a, b, preferred_element_type=F32)


def dot_nt(a, b):
    return lax.dot_general(a, b, (((1,), (1,)), ((), ())), preferred_element_type=F32)


def dot_tn(a, b):
    return lax.dot_general(a, b, (((0,), (0,)), ((), ())), preferred_element_type=F32)


def along_x(block, distance):
    return lax.ppermute(block, "mp", [(i, (i + distance) % SIDE) for i in range(SIDE)])


def along_z(block, distance):
    pairs = [
        (z * SIDE + y, (z + distance) % SIDE * SIDE + y) for z in range(SIDE) for y in range(SIDE)
    ]
    return lax.ppermute(block, "dp", pairs)


def along_y(block, distance):
    pairs = [
        (z * SIDE + y, z * SIDE + (y + distance) % SIDE) for z in range(SIDE) for y in range(SIDE)
    ]
    return lax.ppermute(block, "dp", pairs)


def along_y_of(core, block, distance):
    size = SIDE * SIDE
    pairs = [
        (core * size + z * SIDE + y, core * size + z * SIDE + (y + distance) % SIDE)
        for z in range(SIDE)
        for y in range(SIDE)
    ]
    return lax.ppermute(block, ("segment", "dp"), pairs)


def spread_kernel(routing, place, text, ups, out_text, out_ups, sems):
    core, replica = place[0], place[1]
    copies = []
    for group in range(16):
        slot = jnp.int32(0)
        for j in range(MINE):
            q = routing[(core * 16 + group) * MINE + j]
            slot = jnp.where(lax.shift_right_logical(q, 3) == replica, q & 7, slot)
        for n, (src, dst) in enumerate(((text, out_text), (ups, out_ups))):
            copy = pltpu.make_async_copy(src.at[slot], dst.at[group], sems.at[n, group])
            copy.start()
            copies.append(copy)
    for copy in copies:
        copy.wait()


def spread(routing, place, text, ups):
    shape = jax.ShapeDtypeStruct((16,) + text.shape[1:], text.dtype)
    return pl.pallas_call(
        spread_kernel,
        grid_spec=pltpu.PrefetchScalarGridSpec(
            num_scalar_prefetch=2,
            grid=(1,),
            in_specs=[ANY, ANY],
            out_specs=[ANY, ANY],
            scratch_shapes=[pltpu.SemaphoreType.DMA((2, 16))],
        ),
        out_shape=[shape, shape],
    )(routing, place, text, ups)


def merge_kernel(source, counts, text, image, out):
    row = lax.broadcasted_iota(jnp.int32, (ROWS, text.shape[2]), 0)
    out[0] = jnp.where(row < counts[pl.program_id(0)], image[0], text[0])


def merge(source, counts, text, image):
    columns = text.shape[2]
    block = (1, ROWS, columns)
    return pl.pallas_call(
        merge_kernel,
        grid_spec=pltpu.PrefetchScalarGridSpec(
            num_scalar_prefetch=2,
            grid=(MINE,),
            in_specs=[
                pl.BlockSpec(block, lambda j, source, counts: (source[j], 0, 0)),
                pl.BlockSpec(block, lambda j, source, counts: (j, 0, 0)),
            ],
            out_specs=pl.BlockSpec(block, lambda j, source, counts: (j, 0, 0)),
        ),
        out_shape=jax.ShapeDtypeStruct((MINE, ROWS, columns), text.dtype),
    )(source, counts, text, image).reshape(MINE * ROWS, columns)


def pick_kernel(source, arrived, out):
    out[...] = arrived[...]


def pick(source, arrived):
    columns = arrived.shape[2]
    block = (1, ROWS, columns)
    return pl.pallas_call(
        pick_kernel,
        grid_spec=pltpu.PrefetchScalarGridSpec(
            num_scalar_prefetch=1,
            grid=(MINE,),
            in_specs=[pl.BlockSpec(block, lambda j, source: (source[j], 0, 0))],
            out_specs=pl.BlockSpec(block, lambda j, source: (j, 0, 0)),
        ),
        out_shape=jax.ShapeDtypeStruct((MINE, ROWS, columns), arrived.dtype),
    )(source, arrived).reshape(MINE * ROWS, columns)


def turn_kernel(place, own, other, out, sems):
    core, x = place[0], place[2]
    size = out.shape[2]

    def copy(source, section, d):
        block = lax.rem(x - d + SIDE, SIDE)
        start = pl.multiple_of(block * size, size)
        return pltpu.make_async_copy(
            source.at[pl.ds(start, size)], out.at[section, d], sems.at[section, d]
        )

    for section in range(2):
        for d in range(SIDE):

            @pl.when(core == section)
            def _():
                copy(own, section, d).start()

            @pl.when(core != section)
            def _():
                copy(other, section, d).start()

    for section in range(2):
        for d in range(SIDE):
            copy(own, section, d).wait()


def turn(place, own, other):
    rows, columns = own.shape
    return pl.pallas_call(
        turn_kernel,
        grid_spec=pltpu.PrefetchScalarGridSpec(
            num_scalar_prefetch=1,
            grid=(1,),
            in_specs=[ANY, ANY],
            out_specs=ANY,
            scratch_shapes=[pltpu.SemaphoreType.DMA((2, SIDE))],
        ),
        out_shape=jax.ShapeDtypeStruct((2, SIDE, rows // SIDE, columns), own.dtype),
    )(place, own, other)


def order_kernel(place, in0, in1, in2, in3, out0, out1, out2, out3, sems):
    x, y, z = place[2], place[3], place[4]
    blocks = (in0, in1, in2, in3)
    outs = (out0, out1, out2, out3)
    part = in0.shape[1] // SIDE

    def copy(d, e, j):
        start = pl.multiple_of(lax.rem(y + j, SIDE) * part, part)
        return pltpu.make_async_copy(
            blocks[d].at[:, pl.ds(start, part)],
            outs[e].at[:, pl.ds(j * part, part)],
            sems.at[e, j],
        )

    for e in range(SIDE):
        for d in range(SIDE):

            @pl.when(lax.rem(x - z - e + 2 * SIDE, SIDE) == d)
            def _():
                for j in range(SIDE):
                    copy(d, e, j).start()

    for e in range(SIDE):
        for j in range(SIDE):
            copy(0, e, j).wait()


def order(place, blocks):
    shape = jax.ShapeDtypeStruct(blocks[0].shape, blocks[0].dtype)
    return pl.pallas_call(
        order_kernel,
        grid_spec=pltpu.PrefetchScalarGridSpec(
            num_scalar_prefetch=1,
            grid=(1,),
            in_specs=[ANY] * 4,
            out_specs=[ANY] * 4,
            scratch_shapes=[pltpu.SemaphoreType.DMA((SIDE, SIDE))],
        ),
        out_shape=[shape] * 4,
    )(place, *blocks)


def line_up_kernel(place, arrived, out, sems):
    core, z = place[0], place[4]
    copies = []
    for other in range(2):
        for e in range(SIDE):
            block = lax.rem(core + other, 2) * SIDE + lax.rem(z - e + SIDE, SIDE)
            copy = pltpu.make_async_copy(
                arrived.at[block], out.at[other * SIDE + e], sems.at[other, e]
            )
            copy.start()
            copies.append(copy)
    for copy in copies:
        copy.wait()


def line_up(place, arrived):
    return pl.pallas_call(
        line_up_kernel,
        grid_spec=pltpu.PrefetchScalarGridSpec(
            num_scalar_prefetch=1,
            grid=(1,),
            in_specs=[ANY],
            out_specs=ANY,
            scratch_shapes=[pltpu.SemaphoreType.DMA((2, SIDE))],
        ),
        out_shape=jax.ShapeDtypeStruct(arrived.shape, arrived.dtype),
    )(place, arrived)


def gelu_back(preact, cotangent):
    _, pullback = jax.vjp(jax.nn.gelu, preact)
    return pullback(cotangent)[0]


def on_device(patches, merger_weight, image_counts, routing, text_embed, llm_weight, upstream):
    core = lax.axis_index("segment")
    x = lax.axis_index("mp")
    replica = lax.axis_index("dp")
    z, y = replica // SIDE, replica % SIDE
    place = jnp.stack([core, replica, x, y, z]).astype(jnp.int32)
    group = core * 16 + replica
    columns = merger_weight.shape[1]
    merger = patches.shape[2]

    send_text, send_ups = spread(
        routing,
        place,
        text_embed.reshape(SLOTS, ROWS, columns),
        upstream.reshape(SLOTS, ROWS, columns),
    )
    arrived_text = lax.all_to_all(send_text, "dp", 0, 0, tiled=True)
    own_weight = llm_weight[0]
    other_weight = lax.ppermute(own_weight, "segment", [(0, 1), (1, 0)])
    source = lax.dynamic_slice_in_dim(routing, group * MINE, MINE) // SLOTS
    counts = lax.dynamic_slice_in_dim(image_counts, group * MINE, MINE)

    activated = jax.nn.gelu(patches.astype(F32)).astype(BF).reshape(MINE * ROWS, merger)
    embeds = dot(activated, merger_weight).astype(BF).reshape(MINE, ROWS, columns)
    weights = turn(place, own_weight, other_weight)
    hidden = merge(source, counts, arrived_text, embeds)
    arrived_ups = lax.all_to_all(send_ups, "dp", 0, 0, tiled=True)

    parts = activated.reshape(MINE * ROWS, 8, merger // 8).transpose(1, 0, 2)
    eights = [
        [c * 16 + zz * SIDE + yy for c in range(2) for zz in range(SIDE)] for yy in range(SIDE)
    ]
    act_cols = lax.all_to_all(
        parts, ("segment", "dp"), 0, 0, tiled=True, axis_index_groups=eights
    )
    act_cols = line_up(place, act_cols).reshape(8 * MINE * ROWS, merger // 8)

    saved = []
    rows_of = []
    for section in range(2):
        blocks = [hidden] + [along_x(hidden, d) for d in (1, 2, 3)]
        preact = dot(blocks[0], weights[section, 0])
        for d in (1, 3, 2):
            preact = preact + dot(blocks[d], weights[section, d])
        saved.append(preact)
        ordered = order(place, blocks)
        tokens = [ordered[0]] + [along_z(ordered[e], e) for e in (1, 2, 3)]
        tokens = jnp.concatenate(tokens, axis=0)
        hop = lax.ppermute(tokens, "segment", [(1 - section, section)])
        rows_of.append((tokens, hop))
        if section == 0:
            hidden = (hidden.astype(F32) + jax.nn.gelu(preact)).astype(BF)

    cotangent = pick(source, arrived_ups)
    partials = []
    for section in (1, 0):
        local = gelu_back(saved[section], cotangent.astype(F32)).astype(BF)
        terms = [
            along_x(dot_nt(local, weights[section, SIDE - d]).astype(BF), d) for d in (2, 1, 3)
        ]
        terms.append(dot_nt(local, weights[section, 0]).astype(BF))
        inner = sum(term.astype(F32) for term in terms)
        cotangent = (cotangent.astype(F32) + inner).astype(BF)
        locals_here = [local] + [along_z(local, e) for e in (1, 2, 3)]
        locals_here = jnp.concatenate(locals_here, axis=0)
        hop = lax.ppermute(locals_here, "segment", [(1 - section, section)])
        tokens, tokens_hop = rows_of[section]
        part = dot_tn(tokens, locals_here) + dot_tn(tokens_hop, hop)
        part = part.astype(BF).reshape(SIDE, -1, columns)
        own = part[0].astype(F32)
        for j in (1, 2, 3):
            own = own + along_y_of(section, part[j], j).astype(F32)
        partials.append(own)
    llm_grad = jnp.where(core == 0, partials[1], partials[0])[None]

    position = jnp.arange(MINE * ROWS) % ROWS
    image_rows = position < jnp.repeat(counts, ROWS)
    image_grad = jnp.where(image_rows[:, None], cotangent, jnp.zeros((), BF))
    grads = [image_grad] + [along_z(image_grad, e) for e in (1, 2, 3)]
    grads = jnp.concatenate(grads, axis=0)
    grads_hop = lax.ppermute(grads, "segment", [(0, 1), (1, 0)])
    half = grads.shape[0]
    part = dot_tn(act_cols[:half], grads) + dot_tn(act_cols[half:], grads_hop)
    part = part.astype(BF).reshape(SIDE, -1, columns)

    def toward(j):
        return lax.dynamic_index_in_dim(part, (y + j) % SIDE, 0, keepdims=False)

    merger_grad = toward(0).astype(F32)
    for j in (1, 2, 3):
        merger_grad = merger_grad + along_y(toward(j), j).astype(F32)
    return (llm_grad, merger_grad)


def solution(mesh):
    return jax.shard_map(
        on_device,
        mesh=mesh,
        in_specs=(
            P(("segment", "dp"), None, None),
            P(None, "mp"),
            P(),
            P(),
            P(None, "dp", "mp"),
            P("segment", None, "mp"),
            P(None, "dp", "mp"),
        ),
        out_specs=(P("segment", "dp", "mp"), P(("segment", "dp"), "mp")),
        check_vma=False,
    )
```

```python
import jax
import jax.numpy as jnp
from jax import lax
from jax.experimental import pallas as pl
from jax.experimental.pallas import tpu as pltpu
from jax.sharding import PartitionSpec as P

BF = jnp.bfloat16
F32 = jnp.float32
SIDE = 4
SLOTS = 8
ROWS = 32
MINE = 4
ANY = pl.BlockSpec(memory_space=pl.ANY)


def dot(a, b):
    return jnp.dot(a, b, preferred_element_type=F32)


def dot_nt(a, b):
    return lax.dot_general(a, b, (((1,), (1,)), ((), ())), preferred_element_type=F32)


def dot_tn(a, b):
    return lax.dot_general(a, b, (((0,), (0,)), ((), ())), preferred_element_type=F32)


def along_x(block, distance):
    return lax.ppermute(block, "mp", [(i, (i + distance) % SIDE) for i in range(SIDE)])


def along_z(block, distance):
    pairs = [
        (z * SIDE + y, (z + distance) % SIDE * SIDE + y) for z in range(SIDE) for y in range(SIDE)
    ]
    return lax.ppermute(block, "dp", pairs)


def along_y(block, distance):
    pairs = [
        (z * SIDE + y, z * SIDE + (y + distance) % SIDE) for z in range(SIDE) for y in range(SIDE)
    ]
    return lax.ppermute(block, "dp", pairs)


def along_y_of(core, block, distance):
    size = SIDE * SIDE
    pairs = [
        (core * size + z * SIDE + y, core * size + z * SIDE + (y + distance) % SIDE)
        for z in range(SIDE)
        for y in range(SIDE)
    ]
    return lax.ppermute(block, ("segment", "dp"), pairs)


def spread_kernel(routing, place, slots, out):
    core, replica = place[0], place[1]
    for group in range(16):
        slot = jnp.int32(0)
        for j in range(MINE):
            q = routing[(core * 16 + group) * MINE + j]
            slot = jnp.where(lax.shift_right_logical(q, 3) == replica, q & 7, slot)
        out[group] = slots[slot]


def spread(routing, place, slots):
    shape = (16,) + slots.shape[1:]
    return pl.pallas_call(
        spread_kernel,
        grid_spec=pltpu.PrefetchScalarGridSpec(
            num_scalar_prefetch=2,
            grid=(1,),
            in_specs=[pl.BlockSpec(slots.shape, lambda i, *_: (0, 0, 0))],
            out_specs=pl.BlockSpec(shape, lambda i, *_: (0, 0, 0)),
        ),
        out_shape=jax.ShapeDtypeStruct(shape, slots.dtype),
    )(routing, place, slots)


def merge_kernel(source, counts, text, image, out):
    row = lax.broadcasted_iota(jnp.int32, (ROWS, text.shape[2]), 0)
    out[0] = jnp.where(row < counts[pl.program_id(0)], image[0], text[0])


def merge(source, counts, text, image):
    columns = text.shape[2]
    block = (1, ROWS, columns)
    return pl.pallas_call(
        merge_kernel,
        grid_spec=pltpu.PrefetchScalarGridSpec(
            num_scalar_prefetch=2,
            grid=(MINE,),
            in_specs=[
                pl.BlockSpec(block, lambda j, source, counts: (source[j], 0, 0)),
                pl.BlockSpec(block, lambda j, source, counts: (j, 0, 0)),
            ],
            out_specs=pl.BlockSpec(block, lambda j, source, counts: (j, 0, 0)),
        ),
        out_shape=jax.ShapeDtypeStruct((MINE, ROWS, columns), text.dtype),
    )(source, counts, text, image).reshape(MINE * ROWS, columns)


def pick_kernel(source, arrived, out):
    out[...] = arrived[...]


def pick(source, arrived):
    columns = arrived.shape[2]
    block = (1, ROWS, columns)
    return pl.pallas_call(
        pick_kernel,
        grid_spec=pltpu.PrefetchScalarGridSpec(
            num_scalar_prefetch=1,
            grid=(MINE,),
            in_specs=[pl.BlockSpec(block, lambda j, source: (source[j], 0, 0))],
            out_specs=pl.BlockSpec(block, lambda j, source: (j, 0, 0)),
        ),
        out_shape=jax.ShapeDtypeStruct((MINE, ROWS, columns), arrived.dtype),
    )(source, arrived).reshape(MINE * ROWS, columns)


def turn_kernel(place, own, other, *outs_and_sems):
    outs, sems = outs_and_sems[:-1], outs_and_sems[-1]
    core, x = place[0], place[2]
    size = outs[0].shape[0]

    def copy(source, n):
        block = lax.rem(x - n % SIDE + SIDE, SIDE)
        start = pl.multiple_of(block * size, size)
        return pltpu.make_async_copy(source.at[pl.ds(start, size)], outs[n], sems.at[n])

    for n in range(2 * SIDE):

        @pl.when(core == n // SIDE)
        def _():
            copy(own, n).start()

        @pl.when(core != n // SIDE)
        def _():
            copy(other, n).start()

    for n in range(2 * SIDE):
        copy(own, n).wait()


def turn(place, own, other):
    rows, columns = own.shape
    blocks = pl.pallas_call(
        turn_kernel,
        in_specs=[pl.BlockSpec(memory_space=pltpu.SMEM), ANY, ANY],
        out_specs=[pl.BlockSpec(memory_space=pltpu.VMEM)] * (2 * SIDE),
        scratch_shapes=[pltpu.SemaphoreType.DMA((2 * SIDE,))],
        out_shape=[pltpu.VMEM((rows // SIDE, columns), own.dtype)] * (2 * SIDE),
        compiler_params=pltpu.CompilerParams(vmem_limit_bytes=40 * 1024 * 1024),
    )(place, own, other)
    return (blocks[:SIDE], blocks[SIDE:])


def order_kernel(place, in0, in1, in2, in3, out0, out1, out2, out3):
    x, y, z = place[2], place[3], place[4]
    blocks = (in0, in1, in2, in3)
    outs = (out0, out1, out2, out3)
    part = in0.shape[1] // SIDE
    for e in range(SIDE):
        for d in range(SIDE):

            @pl.when(lax.rem(x - z - e + 2 * SIDE, SIDE) == d)
            def _():
                for j in range(SIDE):
                    start = pl.multiple_of(lax.rem(y + j, SIDE) * part, part)
                    outs[e][:, pl.ds(j * part, part)] = blocks[d][:, pl.ds(start, part)]


def order(place, blocks):
    shape = jax.ShapeDtypeStruct(blocks[0].shape, blocks[0].dtype)
    whole = pl.BlockSpec(memory_space=pltpu.VMEM)
    return pl.pallas_call(
        order_kernel,
        in_specs=[pl.BlockSpec(memory_space=pltpu.SMEM)] + [whole] * SIDE,
        out_specs=[whole] * SIDE,
        out_shape=[shape] * SIDE,
    )(place, *blocks)


def line_up_kernel(place, arrived, out):
    core, z = place[0], place[4]
    for other in range(2):
        for e in range(SIDE):
            block = lax.rem(core + other, 2) * SIDE + lax.rem(z - e + SIDE, SIDE)
            out[other * SIDE + e] = arrived[block]


def line_up(place, arrived):
    whole = pl.BlockSpec(memory_space=pltpu.VMEM)
    return pl.pallas_call(
        line_up_kernel,
        in_specs=[pl.BlockSpec(memory_space=pltpu.SMEM), whole],
        out_specs=whole,
        out_shape=jax.ShapeDtypeStruct(arrived.shape, arrived.dtype),
    )(place, arrived)


def gelu_back(preact, cotangent):
    _, pullback = jax.vjp(jax.nn.gelu, preact)
    return pullback(cotangent)[0]


def on_device(patches, merger_weight, image_counts, routing, text_embed, llm_weight, upstream):
    core = lax.axis_index("segment")
    x = lax.axis_index("mp")
    replica = lax.axis_index("dp")
    z, y = replica // SIDE, replica % SIDE
    place = jnp.stack([core, replica, x, y, z]).astype(jnp.int32)
    group = core * 16 + replica
    columns = merger_weight.shape[1]
    merger = patches.shape[2]

    send_text = spread(routing, place, text_embed.reshape(SLOTS, ROWS, columns))
    arrived_text = lax.all_to_all(send_text, "dp", 0, 0, tiled=True)
    own_weight = llm_weight[0]
    other_weight = lax.ppermute(own_weight, "segment", [(0, 1), (1, 0)])
    source = lax.dynamic_slice_in_dim(routing, group * MINE, MINE) // SLOTS
    counts = lax.dynamic_slice_in_dim(image_counts, group * MINE, MINE)

    activated = jax.nn.gelu(patches.astype(F32)).astype(BF).reshape(MINE * ROWS, merger)
    embeds = dot(activated, merger_weight).astype(BF).reshape(MINE, ROWS, columns)
    weights = turn(place, own_weight, other_weight)
    hidden = merge(source, counts, arrived_text, embeds)
    send_ups = spread(routing, place, upstream.reshape(SLOTS, ROWS, columns))
    arrived_ups = lax.all_to_all(send_ups, "dp", 0, 0, tiled=True)

    parts = activated.reshape(MINE * ROWS, 8, merger // 8).transpose(1, 0, 2)
    eights = [
        [c * 16 + zz * SIDE + yy for c in range(2) for zz in range(SIDE)] for yy in range(SIDE)
    ]
    act_cols = lax.all_to_all(
        parts, ("segment", "dp"), 0, 0, tiled=True, axis_index_groups=eights
    )
    act_cols = line_up(place, act_cols).reshape(8 * MINE * ROWS, merger // 8)

    saved = []
    rows_of = []
    for section in range(2):
        blocks = [hidden] + [along_x(hidden, d) for d in (1, 2, 3)]
        preact = dot(blocks[0], weights[section][0])
        for d in (1, 3, 2):
            preact = preact + dot(blocks[d], weights[section][d])
        saved.append(preact)
        ordered = order(place, blocks)
        tokens = [ordered[0]] + [along_z(ordered[e], e) for e in (1, 2, 3)]
        tokens = jnp.concatenate(tokens, axis=0)
        hop = lax.ppermute(tokens, "segment", [(1 - section, section)])
        rows_of.append((tokens, hop))
        if section == 0:
            hidden = (hidden.astype(F32) + jax.nn.gelu(preact)).astype(BF)

    cotangent = pick(source, arrived_ups)
    partials = []
    for section in (1, 0):
        local = gelu_back(saved[section], cotangent.astype(F32)).astype(BF)
        terms = [
            along_x(dot_nt(local, weights[section][SIDE - d]).astype(BF), d) for d in (2, 1, 3)
        ]
        terms.append(dot_nt(local, weights[section][0]).astype(BF))
        inner = sum(term.astype(F32) for term in terms)
        cotangent = (cotangent.astype(F32) + inner).astype(BF)
        locals_here = [local] + [along_z(local, e) for e in (1, 2, 3)]
        locals_here = jnp.concatenate(locals_here, axis=0)
        hop = lax.ppermute(locals_here, "segment", [(1 - section, section)])
        tokens, tokens_hop = rows_of[section]
        part = dot_tn(tokens, locals_here) + dot_tn(tokens_hop, hop)
        part = part.astype(BF).reshape(SIDE, -1, columns)
        own = part[0].astype(F32)
        for j in (1, 2, 3):
            own = own + along_y_of(section, part[j], j).astype(F32)
        partials.append(own)
    llm_grad = jnp.where(core == 0, partials[1], partials[0])[None]

    position = jnp.arange(MINE * ROWS) % ROWS
    image_rows = position < jnp.repeat(counts, ROWS)
    image_grad = jnp.where(image_rows[:, None], cotangent, jnp.zeros((), BF))
    grads = [image_grad] + [along_z(image_grad, e) for e in (1, 2, 3)]
    grads = jnp.concatenate(grads, axis=0)
    grads_hop = lax.ppermute(grads, "segment", [(0, 1), (1, 0)])
    half = grads.shape[0]
    part = dot_tn(act_cols[:half], grads) + dot_tn(act_cols[half:], grads_hop)
    part = part.astype(BF).reshape(SIDE, -1, columns)

    def toward(j):
        return lax.dynamic_index_in_dim(part, (y + j) % SIDE, 0, keepdims=False)

    merger_grad = toward(0).astype(F32)
    for j in (1, 2, 3):
        merger_grad = merger_grad + along_y(toward(j), j).astype(F32)
    return (llm_grad, merger_grad)


def solution(mesh):
    return jax.shard_map(
        on_device,
        mesh=mesh,
        in_specs=(
            P(("segment", "dp"), None, None),
            P(None, "mp"),
            P(),
            P(),
            P(None, "dp", "mp"),
            P("segment", None, "mp"),
            P(None, "dp", "mp"),
        ),
        out_specs=(P("segment", "dp", "mp"), P(("segment", "dp"), "mp")),
        check_vma=False,
    )
```

```python
import functools

import jax
import jax.numpy as jnp
from jax import lax
from jax.experimental import pallas as pl
from jax.experimental.pallas import tpu as pltpu
from jax.sharding import PartitionSpec as P

BF = jnp.bfloat16
F32 = jnp.float32
SIDE = 4
SLOTS = 8
ROWS = 32
MINE = 4
ANY = pl.BlockSpec(memory_space=pl.ANY)
WHOLE = pl.BlockSpec(memory_space=pltpu.VMEM)
SCALARS = pl.BlockSpec(memory_space=pltpu.SMEM)
SMALL = pltpu.CompilerParams(vmem_limit_bytes=6 * 1024 * 1024)
Z_GROUPS = [[z * SIDE + y for z in range(SIDE)] for y in range(SIDE)]
Y_GROUPS = [[z * SIDE + y for y in range(SIDE)] for z in range(SIDE)]


def dot(a, b):
    return jnp.dot(a, b, preferred_element_type=F32)


def dot_nt(a, b):
    return lax.dot_general(a, b, (((1,), (1,)), ((), ())), preferred_element_type=F32)


def dot_tn(a, b):
    return lax.dot_general(a, b, (((0,), (0,)), ((), ())), preferred_element_type=F32)


def along_x(block, distance):
    return lax.ppermute(block, "mp", [(i, (i + distance) % SIDE) for i in range(SIDE)])


def along_z(block, distance):
    pairs = [
        (z * SIDE + y, (z + distance) % SIDE * SIDE + y) for z in range(SIDE) for y in range(SIDE)
    ]
    return lax.ppermute(block, "dp", pairs)


def along_y(block, distance):
    pairs = [
        (z * SIDE + y, z * SIDE + (y + distance) % SIDE) for z in range(SIDE) for y in range(SIDE)
    ]
    return lax.ppermute(block, "dp", pairs)


def exchange(blocks, groups):
    return lax.all_to_all(blocks, "dp", 0, 0, tiled=True, axis_index_groups=groups)


def swap(block):
    return lax.ppermute(block, "segment", [(0, 1), (1, 0)])


def after(value, *others):
    return lax.optimization_barrier((value,) + others)[0]


def spread_kernel(routing, place, slots, out):
    core, replica = place[0], place[1]
    for group in range(16):
        slot = jnp.int32(0)
        for j in range(MINE):
            q = routing[(core * 16 + group) * MINE + j]
            slot = jnp.where(lax.shift_right_logical(q, 3) == replica, q & 7, slot)
        out[group] = slots[slot]


def spread(routing, place, slots):
    shape = (16,) + slots.shape[1:]
    return pl.pallas_call(
        spread_kernel,
        in_specs=[SCALARS, SCALARS, WHOLE],
        out_specs=WHOLE,
        out_shape=jax.ShapeDtypeStruct(shape, slots.dtype),
        compiler_params=SMALL,
    )(routing, place, slots)


def merge_kernel(routing, counts, place, arrived, *refs):
    image, out, sems = (refs[0] if len(refs) == 3 else None), refs[-2], refs[-1]
    first = (place[0] * 16 + place[1]) * MINE
    copies = []
    for j in range(MINE):
        replica = lax.shift_right_logical(routing[first + j], 3)
        copy = pltpu.make_async_copy(arrived.at[replica], out.at[j], sems.at[j])
        copy.start()
        copies.append(copy)
    for copy in copies:
        copy.wait()
    if image is not None:
        row = lax.broadcasted_iota(jnp.int32, out.shape[1:], 0)
        for j in range(MINE):
            out[j] = jnp.where(row < counts[first + j], image[j], out[j])


def merge(routing, counts, place, arrived, image=None):
    columns = arrived.shape[2]
    operands = (arrived,) if image is None else (arrived, image)
    return pl.pallas_call(
        merge_kernel,
        in_specs=[SCALARS] * 3 + [ANY] + [WHOLE] * (len(operands) - 1),
        out_specs=WHOLE,
        scratch_shapes=[pltpu.SemaphoreType.DMA((MINE,))],
        out_shape=jax.ShapeDtypeStruct((MINE, ROWS, columns), arrived.dtype),
        compiler_params=SMALL,
    )(routing, counts, place, *operands).reshape(MINE * ROWS, columns)


def turn_kernel(place, own, other, *outs_and_sems):
    outs, sems = outs_and_sems[:-1], outs_and_sems[-1]
    core, x = place[0], place[2]
    size = outs[0].shape[0]

    def copy(source, n):
        block = lax.rem(x - n % SIDE + SIDE, SIDE)
        start = pl.multiple_of(block * size, size)
        return pltpu.make_async_copy(source.at[pl.ds(start, size)], outs[n], sems.at[n])

    for n in range(2 * SIDE):

        @pl.when(core == n // SIDE)
        def _():
            copy(own, n).start()

        @pl.when(core != n // SIDE)
        def _():
            copy(other, n).start()

    for n in range(2 * SIDE):
        copy(own, n).wait()


def turn(place, own, other):
    rows, columns = own.shape
    blocks = pl.pallas_call(
        turn_kernel,
        in_specs=[pl.BlockSpec(memory_space=pltpu.SMEM), ANY, ANY],
        out_specs=[pl.BlockSpec(memory_space=pltpu.VMEM)] * (2 * SIDE),
        scratch_shapes=[pltpu.SemaphoreType.DMA((2 * SIDE,))],
        out_shape=[pltpu.VMEM((rows // SIDE, columns), own.dtype)] * (2 * SIDE),
        compiler_params=pltpu.CompilerParams(vmem_limit_bytes=40 * 1024 * 1024),
    )(place, own, other)
    return (blocks[:SIDE], blocks[SIDE:])


def order_kernel(section, place, in0, in1, in2, in3, out):
    x = place[2]
    blocks = (in0, in1, in2, in3)
    part = in0.shape[1] // SIDE
    for owner in range(SIDE):
        for d in range(SIDE):

            @pl.when(lax.rem(x - d + SIDE, SIDE) == owner)
            def _():
                if section == 0:
                    out[owner] = blocks[d][...]
                else:
                    for y in range(SIDE):
                        out[y, :, pl.ds(owner * part, part)] = blocks[d][:, pl.ds(y * part, part)]


def order(section, place, blocks):
    shape = (SIDE,) + blocks[0].shape
    return pl.pallas_call(
        functools.partial(order_kernel, section),
        in_specs=[SCALARS] + [WHOLE] * SIDE,
        out_specs=WHOLE,
        out_shape=jax.ShapeDtypeStruct(shape, blocks[0].dtype),
        compiler_params=SMALL,
    )(place, *blocks)


def line_up_kernel(place, arrived, out):
    core, z = place[0], place[4]
    for other in range(2):
        for e in range(SIDE):
            block = lax.rem(core + other, 2) * SIDE + lax.rem(z - e + SIDE, SIDE)
            out[other * SIDE + e] = arrived[block]


def line_up(place, arrived):
    return pl.pallas_call(
        line_up_kernel,
        in_specs=[SCALARS, WHOLE],
        out_specs=WHOLE,
        out_shape=jax.ShapeDtypeStruct(arrived.shape, arrived.dtype),
        compiler_params=SMALL,
    )(place, arrived)


def gelu_slope(preact):
    _, pullback = jax.vjp(jax.nn.gelu, preact)
    return pullback(jnp.ones_like(preact))[0]


def on_device(patches, merger_weight, image_counts, routing, text_embed, llm_weight, upstream):
    core = lax.axis_index("segment")
    x = lax.axis_index("mp")
    replica = lax.axis_index("dp")
    z, y = replica // SIDE, replica % SIDE
    place = jnp.stack([core, replica, x, y, z]).astype(jnp.int32)
    group = core * 16 + replica
    columns = merger_weight.shape[1]
    merger = patches.shape[2]
    tokens = MINE * ROWS

    own_weight = llm_weight[0]
    other_weight = swap(own_weight)
    send_text = spread(routing, place, text_embed.reshape(SLOTS, ROWS, columns))
    arrived_text = lax.all_to_all(send_text, "dp", 0, 0, tiled=True)

    activated = jax.nn.gelu(patches.astype(F32)).astype(BF).reshape(tokens, merger)
    embeds = dot(activated, merger_weight).astype(BF).reshape(MINE, ROWS, columns)
    act_parts = activated.reshape(tokens, 8, merger // 8).transpose(1, 0, 2)
    send_ups = spread(routing, place, upstream.reshape(SLOTS, ROWS, columns))
    weights = turn(place, own_weight, other_weight)
    arrived_text, embeds, act_parts, send_ups, weights = lax.optimization_barrier(
        (arrived_text, embeds, act_parts, send_ups, weights)
    )
    hidden = merge(routing, image_counts, place, arrived_text, embeds)

    arrived_ups = lax.all_to_all(after(send_ups, hidden), "dp", 0, 0, tiled=True)
    eights = [
        [c * 16 + zz * SIDE + yy for c in range(2) for zz in range(SIDE)] for yy in range(SIDE)
    ]

    slopes = []
    rows_of = []
    for section in range(2):
        blocks = [hidden] + [along_x(hidden, d) for d in (1, 2, 3)]
        preact = dot(blocks[0], weights[section][0])
        for d in (1, 3, 2):
            preact = preact + dot(blocks[d], weights[section][d])
        if section == 0:
            hidden = (hidden.astype(F32) + jax.nn.gelu(preact)).astype(BF)
        slopes.append(gelu_slope(preact))
        rows_of.append((blocks, preact))

    act_cols = lax.all_to_all(
        after(act_parts, hidden), ("segment", "dp"), 0, 0, tiled=True, axis_index_groups=eights
    )
    act_cols = line_up(place, act_cols).reshape(8 * tokens, merger // 8)
    cotangent = merge(routing, image_counts, place, arrived_ups)
    groups = (Z_GROUPS, Y_GROUPS)
    all_rows = [
        exchange(order(section, place, rows_of[section][0]), groups[section]) for section in (0, 1)
    ]
    all_locals = [None, None]
    for section in (1, 0):
        local = (slopes[section] * cotangent.astype(F32)).astype(BF)
        terms = [
            along_x(dot_nt(local, weights[section][SIDE - d]).astype(BF), d) for d in (2, 1, 3)
        ]
        terms.append(dot_nt(local, weights[section][0]).astype(BF))
        inner = sum(term.astype(F32) for term in terms)
        cotangent = (cotangent.astype(F32) + inner).astype(BF)
        copies = jnp.broadcast_to(local[None], (SIDE,) + local.shape)
        all_locals[section] = exchange(copies, groups[section])

    def my_section(pair):
        first, second = (blocks.reshape(SIDE * tokens, columns) for blocks in pair)
        return (
            jnp.where(core == 0, first, second),
            swap(jnp.where(core == 0, second, first)),
        )

    rows, rows_swapped = my_section(all_rows)
    local, local_swapped = my_section(all_locals)
    part = dot_tn(rows, local) + dot_tn(rows_swapped, local_swapped)
    part = part.astype(BF).reshape(SIDE, -1, columns)
    sums = [[c * 16 + n for n in g] for c, gs in ((0, Y_GROUPS), (1, Z_GROUPS)) for g in gs]
    part = lax.all_to_all(part, ("segment", "dp"), 0, 0, tiled=True, axis_index_groups=sums)
    llm_grad = jnp.sum(part.astype(F32), axis=0)[None]

    counts = lax.dynamic_slice_in_dim(image_counts, group * MINE, MINE)
    image_rows = (jnp.arange(ROWS)[None] < counts[:, None]).reshape(tokens)
    image_grad = jnp.where(image_rows[:, None], cotangent, jnp.zeros((), BF))
    grads = [image_grad] + [along_z(image_grad, e) for e in (1, 2, 3)]
    grads = jnp.concatenate(grads, axis=0)
    grads_swapped = swap(grads)
    half = grads.shape[0]
    part = dot_tn(act_cols[:half], grads) + dot_tn(act_cols[half:], grads_swapped)
    part = part.astype(BF).reshape(SIDE, -1, columns)

    def toward(j):
        return lax.dynamic_index_in_dim(part, (y + j) % SIDE, 0, keepdims=False)

    merger_grad = toward(0).astype(F32)
    for j in (1, 2, 3):
        merger_grad = merger_grad + along_y(toward(j), j).astype(F32)
    return (llm_grad, merger_grad)


def solution(mesh):
    return jax.shard_map(
        on_device,
        mesh=mesh,
        in_specs=(
            P(("segment", "dp"), None, None),
            P(None, "mp"),
            P(),
            P(),
            P(None, "dp", "mp"),
            P("segment", None, "mp"),
            P(None, "dp", "mp"),
        ),
        out_specs=(P("segment", "dp", "mp"), P(("segment", "dp"), "mp")),
        check_vma=False,
    )
```

```python
import functools

import jax
import jax.numpy as jnp
from jax import lax
from jax.experimental import pallas as pl
from jax.experimental.pallas import tpu as pltpu
from jax.sharding import PartitionSpec as P

BF = jnp.bfloat16
F32 = jnp.float32
SIDE = 4
SLOTS = 8
ROWS = 32
MINE = 4
FETCH_ORDER = (0, 1, 3, 2)
ANY = pl.BlockSpec(memory_space=pl.ANY)
WHOLE = pl.BlockSpec(memory_space=pltpu.VMEM)
SCALARS = pl.BlockSpec(memory_space=pltpu.SMEM)
SMALL = pltpu.CompilerParams(vmem_limit_bytes=6 * 1024 * 1024)
Z_GROUPS = [[z * SIDE + y for z in range(SIDE)] for y in range(SIDE)]
Y_GROUPS = [[z * SIDE + y for y in range(SIDE)] for z in range(SIDE)]


def dot(a, b):
    return jnp.dot(a, b, preferred_element_type=F32)


def dot_nt(a, b):
    return lax.dot_general(a, b, (((1,), (1,)), ((), ())), preferred_element_type=F32)


def dot_tn(a, b):
    return lax.dot_general(a, b, (((0,), (0,)), ((), ())), preferred_element_type=F32)


def along_x(block, distance):
    return lax.ppermute(block, "mp", [(i, (i + distance) % SIDE) for i in range(SIDE)])


def along_z(block, distance):
    pairs = [
        (z * SIDE + y, (z + distance) % SIDE * SIDE + y) for z in range(SIDE) for y in range(SIDE)
    ]
    return lax.ppermute(block, "dp", pairs)


def along_y(block, distance):
    pairs = [
        (z * SIDE + y, z * SIDE + (y + distance) % SIDE) for z in range(SIDE) for y in range(SIDE)
    ]
    return lax.ppermute(block, "dp", pairs)


def exchange(blocks, groups):
    return lax.all_to_all(blocks, "dp", 0, 0, tiled=True, axis_index_groups=groups)


def swap(block):
    return lax.ppermute(block, "segment", [(0, 1), (1, 0)])


def after(value, *others):
    return lax.optimization_barrier((value,) + others)[0]


def spread_kernel(routing, place, slots, out):
    core, replica = place[0], place[1]
    for group in range(16):
        slot = jnp.int32(0)
        for j in range(MINE):
            q = routing[(core * 16 + group) * MINE + j]
            slot = jnp.where(lax.shift_right_logical(q, 3) == replica, q & 7, slot)
        out[group] = slots[slot]


def spread(routing, place, slots):
    shape = (16,) + slots.shape[1:]
    return pl.pallas_call(
        spread_kernel,
        in_specs=[SCALARS, SCALARS, WHOLE],
        out_specs=WHOLE,
        out_shape=jax.ShapeDtypeStruct(shape, slots.dtype),
        compiler_params=SMALL,
    )(routing, place, slots)


def merge_kernel(routing, counts, place, arrived, *refs):
    image, out, sems = (refs[0] if len(refs) == 3 else None), refs[-2], refs[-1]
    first = (place[0] * 16 + place[1]) * MINE
    copies = []
    for j in range(MINE):
        replica = lax.shift_right_logical(routing[first + j], 3)
        copy = pltpu.make_async_copy(arrived.at[replica], out.at[j], sems.at[j])
        copy.start()
        copies.append(copy)
    for copy in copies:
        copy.wait()
    if image is not None:
        row = lax.broadcasted_iota(jnp.int32, out.shape[1:], 0)
        for j in range(MINE):
            out[j] = jnp.where(row < counts[first + j], image[j], out[j])


def merge(routing, counts, place, arrived, image=None):
    columns = arrived.shape[2]
    operands = (arrived,) if image is None else (arrived, image)
    return pl.pallas_call(
        merge_kernel,
        in_specs=[SCALARS] * 3 + [ANY] + [WHOLE] * (len(operands) - 1),
        out_specs=WHOLE,
        scratch_shapes=[pltpu.SemaphoreType.DMA((MINE,))],
        out_shape=jax.ShapeDtypeStruct((MINE, ROWS, columns), arrived.dtype),
        compiler_params=SMALL,
    )(routing, counts, place, *operands).reshape(MINE * ROWS, columns)


def gelu_parts(x):
    scale = 0.7978845608028654
    t = jnp.tanh(scale * (x + 0.044715 * (x * x * x)))
    cdf = 0.5 * (1.0 + t)
    slope = cdf + 0.5 * x * (1.0 - t * t) * (scale * (1.0 + 3 * 0.044715 * (x * x)))
    return x * cdf, slope


def fetch_weights(section, place, own, other, held, sems):
    core, x = place[0], place[2]
    size = held.shape[1]

    def copy(source, d):
        start = pl.multiple_of(lax.rem(x - d + SIDE, SIDE) * size, size)
        return pltpu.make_async_copy(source.at[pl.ds(start, size)], held.at[d], sems.at[d])

    for d in FETCH_ORDER:

        @pl.when(core == section)
        def _():
            copy(own, d).start()

        @pl.when(core != section)
        def _():
            copy(other, d).start()

    return lambda d: copy(own, d).wait()


def forward_product(wait, held, blocks):
    total = None
    for d in FETCH_ORDER:
        wait(d)
        product = dot(blocks[d][...], held[d])
        total = product if total is None else total + product
    return total


def forward_kernel(place, own, other, b0, b1, b2, b3, hidden, slope, held, sems):
    wait = fetch_weights(0, place, own, other, held, sems)
    activation, slope[...] = gelu_parts(forward_product(wait, held, (b0, b1, b2, b3)))
    hidden[...] = (b0[...].astype(F32) + activation).astype(BF)


def send_terms(local, copies, held, terms, wait=None):
    for n in range(SIDE):
        copies[n] = local
    for d in (2, 1, 3, 0):
        block = (SIDE - d) % SIDE
        if wait is not None:
            wait(block)
        terms[d][...] = dot_nt(local, held[block]).astype(BF)


def middle_kernel(
    place, own, other, b0, b1, b2, b3, upstream, copies, t0, t1, t2, t3, held, sems
):
    wait = fetch_weights(1, place, own, other, held, sems)
    _, slope = gelu_parts(forward_product(wait, held, (b0, b1, b2, b3)))
    local = (slope * upstream[...].astype(F32)).astype(BF)
    send_terms(local, copies, held, (t0, t1, t2, t3))


def summed(cotangent, terms):
    total = terms[0][...].astype(F32)
    for term in terms[1:]:
        total = total + term[...].astype(F32)
    return (cotangent[...].astype(F32) + total).astype(BF)


def backward_kernel(
    place, own, other, r0, r1, r2, r3, upstream, slope, cotangent, copies, t0, t1, t2, t3, held, sems
):
    wait = fetch_weights(0, place, own, other, held, sems)
    now = summed(upstream, (r0, r1, r2, r3))
    cotangent[...] = now
    local = (slope[...] * now.astype(F32)).astype(BF)
    send_terms(local, copies, held, (t0, t1, t2, t3), wait)


def last_kernel(counts, place, r0, r1, r2, r3, cotangent, out):
    now = summed(cotangent, (r0, r1, r2, r3))
    first = (place[0] * 16 + place[1]) * MINE
    row = lax.broadcasted_iota(jnp.int32, (ROWS, now.shape[1]), 0)
    for j in range(MINE):
        rows = pl.ds(j * ROWS, ROWS)
        held = now[j * ROWS : (j + 1) * ROWS]
        out[rows] = jnp.where(row < counts[first + j], held, jnp.zeros_like(held))


def step(kernel, place, own, other, operands, outs):
    rows, columns = own.shape
    return pl.pallas_call(
        kernel,
        in_specs=[SCALARS, ANY, ANY] + [WHOLE] * len(operands),
        out_specs=[WHOLE] * len(outs),
        out_shape=outs,
        scratch_shapes=[
            pltpu.VMEM((SIDE, rows // SIDE, columns), own.dtype),
            pltpu.SemaphoreType.DMA((SIDE,)),
        ],
        compiler_params=pltpu.CompilerParams(vmem_limit_bytes=24 * 1024 * 1024),
    )(place, own, other, *operands)


def weight_grad_kernel(place, *refs):
    operands, out, held, sems = refs[:8], refs[8], refs[9], refs[10]
    for section in range(2):

        @pl.when(place[0] == section)
        def _():
            for n in range(4):
                pltpu.make_async_copy(operands[section * 4 + n], held.at[n], sems.at[n]).start()

    for n in range(4):
        pltpu.make_async_copy(operands[n], held.at[n], sems.at[n]).wait()
    size = held.shape[1] * held.shape[2]
    rows, rows_far, local, local_far = (held[n].reshape(size, held.shape[3]) for n in range(4))
    total = dot_tn(rows, local) + dot_tn(rows_far, local_far)
    out[...] = total.astype(BF).reshape(out.shape)


def weight_grad(place, operands):
    shape = operands[0].shape
    columns = shape[2]
    return pl.pallas_call(
        weight_grad_kernel,
        in_specs=[SCALARS] + [ANY] * 8,
        out_specs=WHOLE,
        out_shape=jax.ShapeDtypeStruct((SIDE, columns // SIDE, columns), BF),
        scratch_shapes=[pltpu.VMEM((4,) + shape, BF), pltpu.SemaphoreType.DMA((4,))],
        compiler_params=pltpu.CompilerParams(vmem_limit_bytes=24 * 1024 * 1024),
    )(place, *operands)


def merger_kernel(place, act, *refs):
    grads, outs, held = refs[:8], refs[8:12], refs[12]
    total = None
    for n in range(8):
        product = dot_tn(act[n], grads[n][...])
        total = product if total is None else total + product
    held[...] = total
    size = outs[0].shape[0]
    for j in range(SIDE):
        start = pl.multiple_of(lax.rem(place[3] + j, SIDE) * size, size)
        outs[j][...] = held[pl.ds(start, size)].astype(BF)


def merger_parts(place, act, grads):
    columns = grads[0].shape[1]
    rows = act.shape[2]
    shape = jax.ShapeDtypeStruct((rows // SIDE, columns), BF)
    return pl.pallas_call(
        merger_kernel,
        in_specs=[SCALARS] + [WHOLE] * 9,
        out_specs=[WHOLE] * SIDE,
        out_shape=[shape] * SIDE,
        scratch_shapes=[pltpu.VMEM((rows, columns), F32)],
        compiler_params=pltpu.CompilerParams(vmem_limit_bytes=16 * 1024 * 1024),
    )(place, act, *grads)


def split_kernel(activated, out):
    size = out.shape[2]
    for n in range(8):
        out[n] = activated[:, n * size : (n + 1) * size]


def split(activated):
    rows, columns = activated.shape
    return pl.pallas_call(
        split_kernel,
        in_specs=[WHOLE],
        out_specs=WHOLE,
        out_shape=jax.ShapeDtypeStruct((8, rows, columns // 8), activated.dtype),
        compiler_params=SMALL,
    )(activated)


def order_kernel(section, place, in0, in1, in2, in3, out):
    x = place[2]
    blocks = (in0, in1, in2, in3)
    part = in0.shape[1] // SIDE
    for owner in range(SIDE):
        for d in range(SIDE):

            @pl.when(lax.rem(x - d + SIDE, SIDE) == owner)
            def _():
                if section == 0:
                    out[owner] = blocks[d][...]
                else:
                    for y in range(SIDE):
                        out[y, :, pl.ds(owner * part, part)] = blocks[d][:, pl.ds(y * part, part)]


def order(section, place, blocks):
    shape = (SIDE,) + blocks[0].shape
    return pl.pallas_call(
        functools.partial(order_kernel, section),
        in_specs=[SCALARS] + [WHOLE] * SIDE,
        out_specs=WHOLE,
        out_shape=jax.ShapeDtypeStruct(shape, blocks[0].dtype),
        compiler_params=SMALL,
    )(place, *blocks)


def line_up_kernel(place, arrived, out):
    core, z = place[0], place[4]
    for other in range(2):
        for e in range(SIDE):
            block = lax.rem(core + other, 2) * SIDE + lax.rem(z - e + SIDE, SIDE)
            out[other * SIDE + e] = arrived[block]


def line_up(place, arrived):
    return pl.pallas_call(
        line_up_kernel,
        in_specs=[SCALARS, WHOLE],
        out_specs=WHOLE,
        out_shape=jax.ShapeDtypeStruct(arrived.shape, arrived.dtype),
        compiler_params=SMALL,
    )(place, arrived)


def on_device(patches, merger_weight, image_counts, routing, text_embed, llm_weight, upstream):
    core = lax.axis_index("segment")
    x = lax.axis_index("mp")
    replica = lax.axis_index("dp")
    z, y = replica // SIDE, replica % SIDE
    place = jnp.stack([core, replica, x, y, z]).astype(jnp.int32)
    columns = merger_weight.shape[1]
    merger = patches.shape[2]
    tokens = MINE * ROWS
    block = jax.ShapeDtypeStruct((tokens, columns), BF)
    block4 = jax.ShapeDtypeStruct((SIDE, tokens, columns), BF)
    groups = (Z_GROUPS, Y_GROUPS)

    own = llm_weight[0]
    other = swap(own)
    send_text = spread(routing, place, text_embed.reshape(SLOTS, ROWS, columns))
    arrived_text = lax.all_to_all(send_text, "dp", 0, 0, tiled=True)
    activated = jax.nn.gelu(patches.astype(F32)).astype(BF).reshape(tokens, merger)
    embeds = dot(activated, merger_weight).astype(BF).reshape(MINE, ROWS, columns)
    act_parts = split(activated)
    send_ups = spread(routing, place, upstream.reshape(SLOTS, ROWS, columns))
    arrived_text, embeds, act_parts, send_ups, other = lax.optimization_barrier(
        (arrived_text, embeds, act_parts, send_ups, other)
    )
    start = merge(routing, image_counts, place, arrived_text, embeds)

    arrived_ups = lax.all_to_all(after(send_ups, start), "dp", 0, 0, tiled=True)
    blocks0 = [start] + [along_x(start, d) for d in (1, 2, 3)]
    hidden, slope = step(
        forward_kernel, place, own, other, blocks0, [block, jax.ShapeDtypeStruct(block.shape, F32)]
    )
    blocks1 = [hidden] + [along_x(hidden, d) for d in (1, 2, 3)]
    rows0 = exchange(order(0, place, blocks0), Z_GROUPS)
    top = merge(routing, image_counts, place, arrived_ups)
    eights = [
        [c * 16 + zz * SIDE + yy for c in range(2) for zz in range(SIDE)] for yy in range(SIDE)
    ]
    act_cols = lax.all_to_all(
        after(act_parts, hidden), ("segment", "dp"), 0, 0, tiled=True, axis_index_groups=eights
    )

    local1, *terms = step(
        middle_kernel, place, own, other, blocks1 + [top], [block4] + [block] * SIDE
    )
    terms = [terms[0]] + [along_x(terms[d], d) for d in (1, 2, 3)]
    rows1 = exchange(order(1, place, blocks1), Y_GROUPS)
    local1 = exchange(local1, Y_GROUPS)

    cotangent, local0, *terms = step(
        backward_kernel,
        place,
        own,
        other,
        terms + [top, slope],
        [block, block4] + [block] * SIDE,
    )
    terms = [terms[0]] + [along_x(terms[d], d) for d in (1, 2, 3)]
    local0 = exchange(local0, Z_GROUPS)
    to_first, to_second = [(1, 0)], [(0, 1)]
    operands = []
    for mine, pairs in (
        (rows0, to_first),
        (local0, to_first),
        (rows1, to_second),
        (local1, to_second),
    ):
        operands.append((mine, lax.ppermute(mine, "segment", pairs)))
    part = weight_grad(
        place, operands[0] + operands[1] + operands[2] + operands[3]
    )
    sums = [[c * 16 + n for n in g] for c, gs in ((0, Y_GROUPS), (1, Z_GROUPS)) for g in gs]
    part = lax.all_to_all(part, ("segment", "dp"), 0, 0, tiled=True, axis_index_groups=sums)
    llm_grad = jnp.sum(part.astype(F32), axis=0)[None]

    grad = pl.pallas_call(
        last_kernel,
        in_specs=[SCALARS, SCALARS] + [WHOLE] * 5,
        out_specs=WHOLE,
        out_shape=block,
        compiler_params=SMALL,
    )(image_counts, place, *terms, cotangent)
    act_cols = line_up(place, act_cols)
    grads = [grad] + [along_z(grad, e) for e in (1, 2, 3)]
    parts = merger_parts(place, act_cols, grads + [swap(g) for g in grads])
    merger_grad = parts[0].astype(F32)
    for j in (1, 2, 3):
        merger_grad = merger_grad + along_y(parts[j], j).astype(F32)
    return (llm_grad, merger_grad)


def solution(mesh):
    return jax.shard_map(
        on_device,
        mesh=mesh,
        in_specs=(
            P(("segment", "dp"), None, None),
            P(None, "mp"),
            P(),
            P(),
            P(None, "dp", "mp"),
            P("segment", None, "mp"),
            P(None, "dp", "mp"),
        ),
        out_specs=(P("segment", "dp", "mp"), P(("segment", "dp"), "mp")),
        check_vma=False,
    )
```

```python
import functools

import jax
import jax.numpy as jnp
from jax import lax
from jax.experimental import pallas as pl
from jax.experimental.pallas import tpu as pltpu
from jax.sharding import PartitionSpec as P

BF = jnp.bfloat16
F32 = jnp.float32
SIDE = 4
SLOTS = 8
ROWS = 32
MINE = 4
FETCH_ORDER = (0, 1, 3, 2)
ANY = pl.BlockSpec(memory_space=pl.ANY)
WHOLE = pl.BlockSpec(memory_space=pltpu.VMEM)
SCALARS = pl.BlockSpec(memory_space=pltpu.SMEM)
LIMIT = pltpu.CompilerParams(vmem_limit_bytes=60 * 1024 * 1024)
Z_GROUPS = [[z * SIDE + y for z in range(SIDE)] for y in range(SIDE)]
Y_GROUPS = [[z * SIDE + y for y in range(SIDE)] for z in range(SIDE)]


def dot(a, b):
    return jnp.dot(a, b, preferred_element_type=F32)


def dot_nt(a, b):
    return lax.dot_general(a, b, (((1,), (1,)), ((), ())), preferred_element_type=F32)


def dot_tn(a, b):
    return lax.dot_general(a, b, (((0,), (0,)), ((), ())), preferred_element_type=F32)


def along_x(block, distance):
    return lax.ppermute(block, "mp", [(i, (i + distance) % SIDE) for i in range(SIDE)])


def along_z(block, distance):
    pairs = [
        (z * SIDE + y, (z + distance) % SIDE * SIDE + y) for z in range(SIDE) for y in range(SIDE)
    ]
    return lax.ppermute(block, "dp", pairs)


def along_y(block, distance):
    pairs = [
        (z * SIDE + y, z * SIDE + (y + distance) % SIDE) for z in range(SIDE) for y in range(SIDE)
    ]
    return lax.ppermute(block, "dp", pairs)


def exchange(blocks, groups):
    return lax.all_to_all(blocks, "dp", 0, 0, tiled=True, axis_index_groups=groups)


def swap(block):
    return lax.ppermute(block, "segment", [(0, 1), (1, 0)])


def after(value, *others):
    return lax.optimization_barrier((value,) + others)[0]


def spread_kernel(routing, place, slots, out):
    core, replica = place[0], place[1]
    for group in range(16):
        slot = jnp.int32(0)
        for j in range(MINE):
            q = routing[(core * 16 + group) * MINE + j]
            slot = jnp.where(lax.shift_right_logical(q, 3) == replica, q & 7, slot)
        out[group] = slots[slot]


def spread(routing, place, slots):
    shape = (16,) + slots.shape[1:]
    return pl.pallas_call(
        spread_kernel,
        in_specs=[SCALARS, SCALARS, WHOLE],
        out_specs=WHOLE,
        out_shape=jax.ShapeDtypeStruct(shape, slots.dtype),
        compiler_params=LIMIT,
    )(routing, place, slots)


def merge_kernel(routing, counts, place, arrived, *refs):
    image, out, sems = (refs[0] if len(refs) == 3 else None), refs[-2], refs[-1]
    first = (place[0] * 16 + place[1]) * MINE
    copies = []
    for j in range(MINE):
        replica = lax.shift_right_logical(routing[first + j], 3)
        copy = pltpu.make_async_copy(arrived.at[replica], out.at[j], sems.at[j])
        copy.start()
        copies.append(copy)
    for copy in copies:
        copy.wait()
    if image is not None:
        row = lax.broadcasted_iota(jnp.int32, out.shape[1:], 0)
        for j in range(MINE):
            out[j] = jnp.where(row < counts[first + j], image[j], out[j])


def merge(routing, counts, place, arrived, image=None):
    columns = arrived.shape[2]
    operands = (arrived,) if image is None else (arrived, image)
    return pl.pallas_call(
        merge_kernel,
        in_specs=[SCALARS] * 3 + [ANY] + [WHOLE] * (len(operands) - 1),
        out_specs=WHOLE,
        scratch_shapes=[pltpu.SemaphoreType.DMA((MINE,))],
        out_shape=jax.ShapeDtypeStruct((MINE, ROWS, columns), arrived.dtype),
        compiler_params=LIMIT,
    )(routing, counts, place, *operands).reshape(MINE * ROWS, columns)


def gelu_parts(x):
    scale = 0.7978845608028654
    t = jnp.tanh(scale * (x + 0.044715 * (x * x * x)))
    cdf = 0.5 * (1.0 + t)
    slope = cdf + 0.5 * x * (1.0 - t * t) * (scale * (1.0 + 3 * 0.044715 * (x * x)))
    return x * cdf, slope


def fetch_weights(section, place, own, other, held, sems):
    core, x = place[0], place[2]
    size = held.shape[1]

    def copy(source, d):
        start = pl.multiple_of(lax.rem(x - d + SIDE, SIDE) * size, size)
        return pltpu.make_async_copy(source.at[pl.ds(start, size)], held.at[d], sems.at[d])

    for d in FETCH_ORDER:

        @pl.when(core == section)
        def _():
            copy(own, d).start()

        @pl.when(core != section)
        def _():
            copy(other, d).start()

    return lambda d: copy(own, d).wait()


def forward_product(wait, held, blocks):
    total = None
    for d in FETCH_ORDER:
        wait(d)
        product = dot(blocks[d][...], held[d])
        total = product if total is None else total + product
    return total


def forward_kernel(place, own, other, b0, b1, b2, b3, hidden, slope, held, sems):
    wait = fetch_weights(0, place, own, other, held, sems)
    activation, slope[...] = gelu_parts(forward_product(wait, held, (b0, b1, b2, b3)))
    hidden[...] = (b0[...].astype(F32) + activation).astype(BF)


def send_terms(local, held, terms, wait=None):
    for d in (2, 1, 3, 0):
        block = (SIDE - d) % SIDE
        if wait is not None:
            wait(block)
        terms[d][...] = dot_nt(local, held[block]).astype(BF)


def middle_kernel(
    place, own, other, b0, b1, b2, b3, upstream, out, t0, t1, t2, t3, held, sems
):
    wait = fetch_weights(1, place, own, other, held, sems)
    _, slope = gelu_parts(forward_product(wait, held, (b0, b1, b2, b3)))
    local = (slope * upstream[...].astype(F32)).astype(BF)
    out[...] = local
    send_terms(local, held, (t0, t1, t2, t3))


def summed(cotangent, terms):
    total = terms[0][...].astype(F32)
    for term in terms[1:]:
        total = total + term[...].astype(F32)
    return (cotangent[...].astype(F32) + total).astype(BF)


def backward_kernel(
    place, own, other, r0, r1, r2, r3, upstream, slope, cotangent, out, t0, t1, t2, t3, held, sems
):
    wait = fetch_weights(0, place, own, other, held, sems)
    now = summed(upstream, (r0, r1, r2, r3))
    cotangent[...] = now
    local = (slope[...] * now.astype(F32)).astype(BF)
    out[...] = local
    send_terms(local, held, (t0, t1, t2, t3), wait)


def last_kernel(counts, place, r0, r1, r2, r3, cotangent, out):
    now = summed(cotangent, (r0, r1, r2, r3))
    first = (place[0] * 16 + place[1]) * MINE
    row = lax.broadcasted_iota(jnp.int32, (ROWS, now.shape[1]), 0)
    for j in range(MINE):
        rows = pl.ds(j * ROWS, ROWS)
        held = now[j * ROWS : (j + 1) * ROWS]
        out[rows] = jnp.where(row < counts[first + j], held, jnp.zeros_like(held))


def step(kernel, place, own, other, operands, outs):
    rows, columns = own.shape
    return pl.pallas_call(
        kernel,
        in_specs=[SCALARS, ANY, ANY] + [WHOLE] * len(operands),
        out_specs=[WHOLE] * len(outs),
        out_shape=outs,
        scratch_shapes=[
            pltpu.VMEM((SIDE, rows // SIDE, columns), own.dtype),
            pltpu.SemaphoreType.DMA((SIDE,)),
        ],
        compiler_params=LIMIT,
    )(place, own, other, *operands)


def weight_grad_kernel(place, rows0, rows0_far, both1, both1_far, *refs):
    locals0, out, rows, local, sems = refs[:8], refs[8], refs[9], refs[10], refs[11]
    z = place[4]
    count = rows0.shape[1]

    def copy(source, to, n, which):
        return pltpu.make_async_copy(source, to.at[n], sems.at[which, n])

    @pl.when(place[0] == 0)
    def _():
        for far, source in enumerate((rows0, rows0_far)):
            for e in range(SIDE):
                n = far * SIDE + e
                copy(source.at[lax.rem(z - e + SIDE, SIDE)], rows, n, 0).start()
                copy(locals0[n], local, n, 1).start()

    @pl.when(place[0] == 1)
    def _():
        for far, source in enumerate((both1, both1_far)):
            for e in range(SIDE):
                n = far * SIDE + e
                copy(source.at[e, pl.ds(0, count)], rows, n, 0).start()
                copy(source.at[e, pl.ds(count, count)], local, n, 1).start()

    for n in range(2 * SIDE):
        copy(rows0.at[0], rows, n, 0).wait()
        copy(rows0.at[0], local, n, 1).wait()
    columns = out.shape[2]
    total = dot_tn(rows[...].reshape(-1, columns), local[...].reshape(-1, columns))
    out[...] = total.astype(BF).reshape(out.shape)


def weight_grad(place, rows0, rows0_far, both1, both1_far, locals0):
    _, count, columns = rows0.shape
    held = pltpu.VMEM((2 * SIDE, count, columns), BF)
    return pl.pallas_call(
        weight_grad_kernel,
        in_specs=[SCALARS] + [ANY] * 12,
        out_specs=WHOLE,
        out_shape=jax.ShapeDtypeStruct((SIDE, columns // SIDE, columns), BF),
        scratch_shapes=[held, held, pltpu.SemaphoreType.DMA((2, 2 * SIDE))],
        compiler_params=LIMIT,
    )(place, rows0, rows0_far, both1, both1_far, *locals0)


def merger_kernel(place, act, *refs):
    grads, outs, held = refs[:8], refs[8:12], refs[12]
    core, z = place[0], place[4]
    total = None
    for far in range(2):
        for e in range(SIDE):
            n = lax.rem(core + far, 2) * SIDE + lax.rem(z - e + SIDE, SIDE)
            product = dot(act[n], grads[far * SIDE + e][...])
            total = product if total is None else total + product
    held[...] = total
    size = outs[0].shape[0]
    for j in range(SIDE):
        start = pl.multiple_of(lax.rem(place[3] + j, SIDE) * size, size)
        outs[j][...] = held[pl.ds(start, size)].astype(BF)


def merger_parts(place, act, grads):
    columns = grads[0].shape[1]
    rows = act.shape[1]
    shape = jax.ShapeDtypeStruct((rows // SIDE, columns), BF)
    return pl.pallas_call(
        merger_kernel,
        in_specs=[SCALARS] + [WHOLE] * 9,
        out_specs=[WHOLE] * SIDE,
        out_shape=[shape] * SIDE,
        scratch_shapes=[pltpu.VMEM((rows, columns), F32)],
        compiler_params=LIMIT,
    )(place, act, *grads)


def order_kernel(section, place, in0, in1, in2, in3, *refs):
    out = refs[-1]
    x = place[2]
    blocks = (in0, in1, in2, in3)
    rows, columns = in0.shape
    part = columns // SIDE
    for owner in range(SIDE):
        for d in range(SIDE):

            @pl.when(lax.rem(x - d + SIDE, SIDE) == owner)
            def _():
                if section == 0:
                    out[owner] = blocks[d][...]
                else:
                    for y in range(SIDE):
                        out[y, pl.ds(0, rows), pl.ds(owner * part, part)] = blocks[d][
                            :, pl.ds(y * part, part)
                        ]

    if section == 1:
        for y in range(SIDE):
            out[y, pl.ds(rows, rows)] = refs[0][...]


def order(section, place, operands):
    rows, columns = operands[0].shape
    return pl.pallas_call(
        functools.partial(order_kernel, section),
        in_specs=[SCALARS] + [WHOLE] * len(operands),
        out_specs=WHOLE,
        out_shape=jax.ShapeDtypeStruct((SIDE, rows * (section + 1), columns), BF),
        compiler_params=LIMIT,
    )(place, *operands)


def on_device(patches, merger_weight, image_counts, routing, text_embed, llm_weight, upstream):
    core = lax.axis_index("segment")
    x = lax.axis_index("mp")
    replica = lax.axis_index("dp")
    z, y = replica // SIDE, replica % SIDE
    place = jnp.stack([core, replica, x, y, z]).astype(jnp.int32)
    columns = merger_weight.shape[1]
    merger = patches.shape[2]
    tokens = MINE * ROWS
    block = jax.ShapeDtypeStruct((tokens, columns), BF)

    own = llm_weight[0]
    other = swap(own)
    send_text = spread(routing, place, text_embed.reshape(SLOTS, ROWS, columns))
    arrived_text = lax.all_to_all(send_text, "dp", 0, 0, tiled=True)
    activated = jax.nn.gelu(patches.astype(F32)).astype(BF).reshape(tokens, merger)
    embeds = dot(activated, merger_weight).astype(BF).reshape(MINE, ROWS, columns)
    act_parts = activated.T.reshape(8, merger // 8, tokens)
    send_ups = spread(routing, place, upstream.reshape(SLOTS, ROWS, columns))
    arrived_ups = lax.all_to_all(after(send_ups, embeds), "dp", 0, 0, tiled=True)
    arrived_text, embeds, act_parts, other = lax.optimization_barrier(
        (arrived_text, embeds, act_parts, other)
    )
    start = merge(routing, image_counts, place, arrived_text, embeds)

    blocks0 = [start] + [along_x(start, d) for d in (1, 2, 3)]
    eights = [
        [c * 16 + zz * SIDE + yy for c in range(2) for zz in range(SIDE)] for yy in range(SIDE)
    ]
    act_cols = lax.all_to_all(
        after(act_parts, blocks0[1]), ("segment", "dp"), 0, 0, tiled=True, axis_index_groups=eights
    )
    hidden, slope = step(
        forward_kernel, place, own, other, blocks0, [block, jax.ShapeDtypeStruct(block.shape, F32)]
    )
    blocks1 = [hidden] + [along_x(hidden, d) for d in (1, 2, 3)]
    rows0 = exchange(after(order(0, place, blocks0), blocks1[1]), Z_GROUPS)
    top = merge(routing, image_counts, place, arrived_ups)

    local1, *terms = step(
        middle_kernel, place, own, other, blocks1 + [top], [block] + [block] * SIDE
    )
    terms = [terms[0]] + [along_x(terms[d], d) for d in (1, 2, 3)]
    both1 = order(1, place, blocks1 + [local1])
    both1 = exchange(after(both1, terms[1]), Y_GROUPS)

    cotangent, local0, *terms = step(
        backward_kernel, place, own, other, terms + [top, slope], [block] * (2 + SIDE)
    )
    terms = [terms[0]] + [along_x(terms[d], d) for d in (1, 2, 3)]
    to_first, to_second = [(1, 0)], [(0, 1)]
    rows0_far = lax.ppermute(rows0, "segment", to_first)
    both1_far = lax.ppermute(both1, "segment", to_second)
    locals0 = [local0] + [along_z(local0, e) for e in (1, 2, 3)]
    locals0 += [lax.ppermute(value, "segment", to_first) for value in locals0]
    part = weight_grad(place, rows0, rows0_far, both1, both1_far, locals0)
    sums = [[c * 16 + n for n in g] for c, gs in ((0, Y_GROUPS), (1, Z_GROUPS)) for g in gs]
    part = lax.all_to_all(part, ("segment", "dp"), 0, 0, tiled=True, axis_index_groups=sums)
    llm_grad = jnp.sum(part.astype(F32), axis=0)[None]

    grad = pl.pallas_call(
        last_kernel,
        in_specs=[SCALARS, SCALARS] + [WHOLE] * 5,
        out_specs=WHOLE,
        out_shape=block,
        compiler_params=LIMIT,
    )(image_counts, place, *terms, cotangent)
    grads = [grad] + [along_z(grad, e) for e in (1, 2, 3)]
    parts = merger_parts(place, act_cols, grads + [swap(g) for g in grads])
    merger_grad = parts[0].astype(F32)
    for j in (1, 2, 3):
        merger_grad = merger_grad + along_y(parts[j], j).astype(F32)
    return (llm_grad, merger_grad)


def solution(mesh):
    return jax.shard_map(
        on_device,
        mesh=mesh,
        in_specs=(
            P(("segment", "dp"), None, None),
            P(None, "mp"),
            P(),
            P(),
            P(None, "dp", "mp"),
            P("segment", None, "mp"),
            P(None, "dp", "mp"),
        ),
        out_specs=(P("segment", "dp", "mp"), P(("segment", "dp"), "mp")),
        check_vma=False,
    )
```

```python
import functools

import jax
import jax.numpy as jnp
from jax import lax
from jax.experimental import pallas as pl
from jax.experimental.pallas import tpu as pltpu
from jax.sharding import PartitionSpec as P

BF = jnp.bfloat16
F32 = jnp.float32
SIDE = 4
SLOTS = 8
ROWS = 32
MINE = 4
FETCH_ORDER = (0, 1, 3, 2)
ANY = pl.BlockSpec(memory_space=pl.ANY)
WHOLE = pl.BlockSpec(memory_space=pltpu.VMEM)
SCALARS = pl.BlockSpec(memory_space=pltpu.SMEM)
SMALL = pltpu.CompilerParams(vmem_limit_bytes=8 * 1024 * 1024)
ORDER = pltpu.CompilerParams(vmem_limit_bytes=12 * 1024 * 1024)
LIMIT = pltpu.CompilerParams(vmem_limit_bytes=60 * 1024 * 1024)
Z_GROUPS = [[z * SIDE + y for z in range(SIDE)] for y in range(SIDE)]
Y_GROUPS = [[z * SIDE + y for y in range(SIDE)] for z in range(SIDE)]


def dot(a, b):
    return jnp.dot(a, b, preferred_element_type=F32)


def dot_nt(a, b):
    return lax.dot_general(a, b, (((1,), (1,)), ((), ())), preferred_element_type=F32)


def dot_tn(a, b):
    return lax.dot_general(a, b, (((0,), (0,)), ((), ())), preferred_element_type=F32)


def along_x(block, distance):
    return lax.ppermute(block, "mp", [(i, (i + distance) % SIDE) for i in range(SIDE)])


def along_z(block, distance):
    pairs = [
        (z * SIDE + y, (z + distance) % SIDE * SIDE + y) for z in range(SIDE) for y in range(SIDE)
    ]
    return lax.ppermute(block, "dp", pairs)


def along_y(block, distance):
    pairs = [
        (z * SIDE + y, z * SIDE + (y + distance) % SIDE) for z in range(SIDE) for y in range(SIDE)
    ]
    return lax.ppermute(block, "dp", pairs)


def along_mine(block, distance):
    pairs = []
    for z in range(SIDE):
        for y in range(SIDE):
            here = z * SIDE + y
            pairs.append((here, (z + distance) % SIDE * SIDE + y))
            pairs.append((16 + here, 16 + z * SIDE + (y + distance) % SIDE))
    return lax.ppermute(block, ("segment", "dp"), pairs)


def swap(block):
    return lax.ppermute(block, "segment", [(0, 1), (1, 0)])


def after(value, *others):
    return lax.optimization_barrier((value,) + others)[0]


def spread_kernel(routing, place, slots, out):
    core, replica = place[0], place[1]
    for group in range(16):
        slot = jnp.int32(0)
        for j in range(MINE):
            q = routing[(core * 16 + group) * MINE + j]
            slot = jnp.where(lax.shift_right_logical(q, 3) == replica, q & 7, slot)
        out[group] = slots[slot]


def spread(routing, place, slots):
    shape = (16,) + slots.shape[1:]
    return pl.pallas_call(
        spread_kernel,
        in_specs=[SCALARS, SCALARS, WHOLE],
        out_specs=WHOLE,
        out_shape=jax.ShapeDtypeStruct(shape, slots.dtype),
        compiler_params=LIMIT,
    )(routing, place, slots)


def merge_kernel(routing, counts, place, arrived, image, out, sems):
    first = (place[0] * 16 + place[1]) * MINE
    copies = []
    for j in range(MINE):
        replica = lax.shift_right_logical(routing[first + j], 3)
        copy = pltpu.make_async_copy(arrived.at[replica], out.at[j], sems.at[j])
        copy.start()
        copies.append(copy)
    row = lax.broadcasted_iota(jnp.int32, out.shape[1:], 0)
    for j in range(MINE):
        copies[j].wait()
        out[j] = jnp.where(row < counts[first + j], image[j], out[j])


def merge(routing, counts, place, arrived, image):
    columns = arrived.shape[2]
    return pl.pallas_call(
        merge_kernel,
        in_specs=[SCALARS] * 3 + [ANY, WHOLE],
        out_specs=WHOLE,
        scratch_shapes=[pltpu.SemaphoreType.DMA((MINE,))],
        out_shape=jax.ShapeDtypeStruct((MINE, ROWS, columns), arrived.dtype),
        compiler_params=LIMIT,
    )(routing, counts, place, arrived, image).reshape(MINE * ROWS, columns)


def pick_kernel(routing, place, arrived, out, sems):
    first = (place[0] * 16 + place[1]) * MINE
    copies = []
    for j in range(MINE):
        replica = lax.shift_right_logical(routing[first + j], 3)
        copy = pltpu.make_async_copy(arrived.at[replica], out.at[j], sems.at[j])
        copy.start()
        copies.append(copy)
    for copy in copies:
        copy.wait()


def pick(routing, place, arrived):
    columns = arrived.shape[2]
    return pl.pallas_call(
        pick_kernel,
        in_specs=[SCALARS] * 2 + [ANY],
        out_specs=WHOLE,
        scratch_shapes=[pltpu.SemaphoreType.DMA((MINE,))],
        out_shape=jax.ShapeDtypeStruct((MINE, ROWS, columns), arrived.dtype),
        compiler_params=SMALL,
    )(routing, place, arrived).reshape(MINE * ROWS, columns)


def gelu_parts(x):
    scale = 0.7978845608028654
    t = jnp.tanh(scale * (x + 0.044715 * (x * x * x)))
    cdf = 0.5 * (1.0 + t)
    slope = cdf + 0.5 * x * (1.0 - t * t) * (scale * (1.0 + 3 * 0.044715 * (x * x)))
    return x * cdf, slope


def fetch_weights(section, place, own, other, held, sems):
    core, x = place[0], place[2]
    size = held.shape[1]

    def copy(source, d):
        start = pl.multiple_of(lax.rem(x - d + SIDE, SIDE) * size, size)
        return pltpu.make_async_copy(source.at[pl.ds(start, size)], held.at[d], sems.at[d])

    for d in FETCH_ORDER:

        @pl.when(core == section)
        def _():
            copy(own, d).start()

        @pl.when(core != section)
        def _():
            copy(other, d).start()

    return lambda d: copy(own, d).wait()


def forward_product(wait, held, blocks):
    total = None
    for d in FETCH_ORDER:
        wait(d)
        product = dot(blocks[d][...], held[d][...])
        total = product if total is None else total + product
    return total


def send_terms(local, held, put, first, wait=None):
    for d in (2, 1, 3, 0):
        block = (SIDE - d) % SIDE
        if wait is not None:
            wait(block)
        put(first + d, dot_nt(local, held[block][...]).astype(BF))


def forward_body(wait, held, blocks, put):
    activation, slope = gelu_parts(forward_product(wait, held, blocks))
    put(0, (blocks[0][...].astype(F32) + activation).astype(BF))
    put(1, slope)


def middle_body(wait, held, operands, put):
    _, slope = gelu_parts(forward_product(wait, held, operands[:SIDE]))
    local = (slope * operands[SIDE][...].astype(F32)).astype(BF)
    put(0, local)
    send_terms(local, held, put, 1)


def summed(cotangent, terms):
    total = terms[0][...].astype(F32)
    for term in terms[1:]:
        total = total + term[...].astype(F32)
    return (cotangent[...].astype(F32) + total).astype(BF)


def backward_body(wait, held, operands, put):
    upstream, slope, local1, place = operands[SIDE:]
    now = summed(upstream, operands[:SIDE])
    put(0, now)
    local = (slope[...] * now.astype(F32)).astype(BF)
    first = place[0] == 0
    put(1, jnp.where(first, local, local1[...]))
    put(2, jnp.where(first, local1[...], local))
    send_terms(local, held, put, 3, wait)


def step_kernel(body, section, count, outs, place, own, other, *refs):
    sources, targets = refs[:count], refs[count : count + outs]
    operands = refs[count + outs : 2 * count + outs]
    results = refs[2 * count + outs : 2 * (count + outs)]
    held, weight_sems, in_sems, out_sems = refs[2 * (count + outs) :]
    copies = [
        pltpu.make_async_copy(sources[n], operands[n], in_sems.at[n]) for n in range(count)
    ]
    for copy in copies:
        copy.start()
    wait = fetch_weights(section, place, own, other, held, weight_sems)
    for copy in copies:
        copy.wait()
    out_copies = []

    def put(n, value):
        results[n][...] = value
        copy = pltpu.make_async_copy(results[n], targets[n], out_sems.at[n])
        copy.start()
        out_copies.append(copy)

    body(wait, held, operands, put)
    for copy in out_copies:
        copy.wait()


def step(body, section, place, own, other, operands, outs):
    rows, columns = own.shape
    count = len(operands)
    return pl.pallas_call(
        functools.partial(step_kernel, body, section, count, len(outs)),
        in_specs=[SCALARS] + [ANY] * (2 + count),
        out_specs=[ANY] * len(outs),
        out_shape=outs,
        scratch_shapes=[
            *(pltpu.VMEM(value.shape, value.dtype) for value in list(operands) + list(outs)),
            pltpu.VMEM((SIDE, rows // SIDE, columns), own.dtype),
            pltpu.SemaphoreType.DMA((SIDE,)),
            pltpu.SemaphoreType.DMA((count,)),
            pltpu.SemaphoreType.DMA((len(outs),)),
        ],
        compiler_params=LIMIT,
    )(place, own, other, *operands)


def turn_kernel(place, own, other, *outs_and_sems):
    outs, sems = outs_and_sems[:-1], outs_and_sems[-1]
    core, x = place[0], place[2]
    size = outs[0].shape[0]

    def copy(source, n):
        block = lax.rem(x - n % SIDE + SIDE, SIDE)
        start = pl.multiple_of(block * size, size)
        return pltpu.make_async_copy(source.at[pl.ds(start, size)], outs[n], sems.at[n])

    for n in range(2 * SIDE):

        @pl.when(core == n // SIDE)
        def _():
            copy(own, n).start()

        @pl.when(core != n // SIDE)
        def _():
            copy(other, n).start()

    for n in range(2 * SIDE):
        copy(own, n).wait()


def turn(place, own, other):
    rows, columns = own.shape
    blocks = pl.pallas_call(
        turn_kernel,
        in_specs=[pl.BlockSpec(memory_space=pltpu.SMEM), ANY, ANY],
        out_specs=[pl.BlockSpec(memory_space=pltpu.VMEM)] * (2 * SIDE),
        scratch_shapes=[pltpu.SemaphoreType.DMA((2 * SIDE,))],
        out_shape=[pltpu.VMEM((rows // SIDE, columns), own.dtype)] * (2 * SIDE),
        compiler_params=SMALL,
    )(place, own, other)
    return (blocks[:SIDE], blocks[SIDE:])


def held_kernel(body, count, outs, *refs):
    weights, operands, results = refs[:SIDE], refs[SIDE : SIDE + count], refs[SIDE + count :]

    def put(n, value):
        results[n][...] = value

    body(lambda d: None, weights, operands, put)


def held_step(body, weights, operands, outs):
    count = len(operands)
    return pl.pallas_call(
        functools.partial(held_kernel, body, count, len(outs)),
        in_specs=[
            SCALARS if value.dtype == jnp.int32 else WHOLE for value in list(weights) + operands
        ],
        out_specs=[WHOLE] * len(outs),
        out_shape=outs,
        compiler_params=pltpu.CompilerParams(vmem_limit_bytes=16 * 1024 * 1024),
    )(*weights, *operands)


def last_kernel(counts, place, r0, r1, r2, r3, cotangent, out):
    now = summed(cotangent, (r0, r1, r2, r3))
    first = (place[0] * 16 + place[1]) * MINE
    row = lax.broadcasted_iota(jnp.int32, (ROWS, now.shape[1]), 0)
    for j in range(MINE):
        rows = pl.ds(j * ROWS, ROWS)
        held = now[j * ROWS : (j + 1) * ROWS]
        out[rows] = jnp.where(row < counts[first + j], held, jnp.zeros_like(held))


def weight_grad_kernel(*refs):
    rows, local, out = refs[:SIDE], refs[SIDE : 2 * SIDE], refs[2 * SIDE]
    total = None
    for n in range(SIDE):
        product = dot_tn(rows[n][...], local[n][...])
        total = product if total is None else total + product
    out[...] = total.astype(BF).reshape(out.shape)


def weight_grad(rows, local):
    columns = local[0].shape[1]
    return pl.pallas_call(
        weight_grad_kernel,
        in_specs=[WHOLE] * (2 * SIDE),
        out_specs=WHOLE,
        out_shape=jax.ShapeDtypeStruct((SIDE, columns // SIDE, columns), BF),
        compiler_params=LIMIT,
    )(*rows, *local)


def merger_kernel(place, act, *refs):
    grads, outs, held = refs[:8], refs[8:12], refs[12]
    core, z = place[0], place[4]
    total = None
    for far in range(2):
        for e in range(SIDE):
            n = lax.rem(core + far, 2) * SIDE + lax.rem(z - e + SIDE, SIDE)
            product = dot(act[n], grads[far * SIDE + e][...])
            total = product if total is None else total + product
    held[...] = total
    size = outs[0].shape[0]
    for j in range(SIDE):
        start = pl.multiple_of(lax.rem(place[3] + j, SIDE) * size, size)
        outs[j][...] = held[pl.ds(start, size)].astype(BF)


def merger_parts(place, act, grads):
    columns = grads[0].shape[1]
    rows = act.shape[1]
    shape = jax.ShapeDtypeStruct((rows // SIDE, columns), BF)
    return pl.pallas_call(
        merger_kernel,
        in_specs=[SCALARS] + [WHOLE] * 9,
        out_specs=[WHOLE] * SIDE,
        out_shape=[shape] * SIDE,
        scratch_shapes=[pltpu.VMEM((rows, columns), F32)],
        compiler_params=LIMIT,
    )(place, act, *grads)


def order_kernel(place, *refs):
    blocks, keep, give = refs[: 2 * SIDE], refs[2 * SIDE], refs[2 * SIDE + 1]
    core, x, y, z = place[0], place[2], place[3], place[4]
    part = blocks[0].shape[1] // SIDE

    def write(section, out):
        for d in range(SIDE):
            block = blocks[section * SIDE + d]
            if section == 0:
                out[lax.rem(x - d - z + 2 * SIDE, SIDE)] = block[...]
            else:
                to = pl.ds(pl.multiple_of(lax.rem(x - d + SIDE, SIDE) * part, part), part)
                for e in range(SIDE):
                    of = pl.ds(pl.multiple_of(lax.rem(y + e, SIDE) * part, part), part)
                    out[e, :, to] = block[:, of]

    @pl.when(core == 0)
    def _():
        write(0, keep)
        write(1, give)

    @pl.when(core == 1)
    def _():
        write(1, keep)
        write(0, give)


def order(place, blocks):
    shape = jax.ShapeDtypeStruct((SIDE,) + blocks[0].shape, BF)
    return pl.pallas_call(
        order_kernel,
        in_specs=[SCALARS] + [WHOLE] * (2 * SIDE),
        out_specs=[WHOLE] * 2,
        out_shape=[shape] * 2,
        compiler_params=ORDER,
    )(place, *blocks)


def pair_kernel(keep, far, *outs):
    rows = keep.shape[1]
    for n, out in enumerate(outs):
        out[pl.ds(0, rows)] = keep[n]
        out[pl.ds(rows, rows)] = far[n]


def pair(keep, far):
    count, rows, columns = keep.shape
    return pl.pallas_call(
        pair_kernel,
        in_specs=[WHOLE] * 2,
        out_specs=[WHOLE] * count,
        out_shape=[jax.ShapeDtypeStruct((2 * rows, columns), BF)] * count,
        compiler_params=ORDER,
    )(keep, far)


def on_device(patches, merger_weight, image_counts, routing, text_embed, llm_weight, upstream):
    core = lax.axis_index("segment")
    x = lax.axis_index("mp")
    replica = lax.axis_index("dp")
    z, y = replica // SIDE, replica % SIDE
    place = jnp.stack([core, replica, x, y, z]).astype(jnp.int32)
    columns = merger_weight.shape[1]
    merger = patches.shape[2]
    tokens = MINE * ROWS
    block = jax.ShapeDtypeStruct((tokens, columns), BF)

    own = llm_weight[0]
    other = swap(own)
    send_text = spread(routing, place, text_embed.reshape(SLOTS, ROWS, columns))
    arrived_text = lax.all_to_all(send_text, "dp", 0, 0, tiled=True)
    activated = jax.nn.gelu(patches.astype(F32)).astype(BF).reshape(tokens, merger)
    embeds = dot(activated, merger_weight).astype(BF).reshape(MINE, ROWS, columns)
    send_ups = spread(routing, place, upstream.reshape(SLOTS, ROWS, columns))
    act_parts = activated.T.reshape(8, merger // 8, tokens)
    arrived_text, embeds, act_parts, send_ups, other = lax.optimization_barrier(
        (arrived_text, embeds, act_parts, send_ups, other)
    )
    start = merge(routing, image_counts, place, arrived_text, embeds)

    blocks0 = [start] + [along_x(start, d) for d in (1, 2, 3)]
    arrived_ups = lax.all_to_all(after(send_ups, start), "dp", 0, 0, tiled=True)
    hidden, slope = step(
        forward_body, 0, place, own, other, blocks0, [block, jax.ShapeDtypeStruct(block.shape, F32)]
    )

    blocks1 = [hidden] + [along_x(hidden, d) for d in (1, 2, 3)]
    top = pick(routing, place, arrived_ups)
    weights = turn(place, own, after(other, top))
    local1, *terms = held_step(middle_body, weights[1], blocks1 + [top], [block] * 5)

    terms = [terms[0]] + [along_x(terms[d], d) for d in (1, 2, 3)]
    keep, give = order(place, [after(blocks0[0], local1)] + blocks0[1:] + blocks1)
    rows = pair(keep, swap(give))
    rows = [rows[0]] + [along_mine(rows[e], e) for e in (1, 2, 3)]
    cotangent, keep, give, *sends = held_step(
        backward_body, weights[0], terms + [top, slope, local1, place], [block] * 7
    )

    ends = [sends[0]] + [along_x(sends[d], d) for d in (1, 2, 3)]
    local = pair(keep[None], swap(give)[None])[0]
    local = [local] + [along_mine(local, e) for e in (1, 2, 3)]
    eights = [
        [c * 16 + zz * SIDE + yy for c in range(2) for zz in range(SIDE)] for yy in range(SIDE)
    ]
    act_cols = lax.all_to_all(
        after(act_parts, cotangent), ("segment", "dp"), 0, 0, tiled=True, axis_index_groups=eights
    )
    grad = pl.pallas_call(
        last_kernel,
        in_specs=[SCALARS, SCALARS] + [WHOLE] * 5,
        out_specs=WHOLE,
        out_shape=block,
        compiler_params=SMALL,
    )(image_counts, place, *ends, after(cotangent, *rows[1:], *local[1:]))
    going = grad
    grads = [grad] + [along_z(going, e) for e in (1, 2, 3)]

    part = weight_grad([after(rows[0], grad)] + rows[1:], local)
    sums = [[c * 16 + n for n in g] for c, gs in ((0, Y_GROUPS), (1, Z_GROUPS)) for g in gs]
    part = lax.all_to_all(part, ("segment", "dp"), 0, 0, tiled=True, axis_index_groups=sums)
    llm_grad = jnp.sum(part.astype(F32), axis=0)[None]

    parts = merger_parts(place, act_cols, grads + [swap(g) for g in grads])
    merger_grad = parts[0].astype(F32)
    for j in (1, 2, 3):
        merger_grad = merger_grad + along_y(parts[j], j).astype(F32)
    return (llm_grad, merger_grad)


def solution(mesh):
    return jax.shard_map(
        on_device,
        mesh=mesh,
        in_specs=(
            P(("segment", "dp"), None, None),
            P(None, "mp"),
            P(),
            P(),
            P(None, "dp", "mp"),
            P("segment", None, "mp"),
            P(None, "dp", "mp"),
        ),
        out_specs=(P("segment", "dp", "mp"), P(("segment", "dp"), "mp")),
        check_vma=False,
    )
```

```python
import functools

import jax
import jax.numpy as jnp
from jax import lax
from jax.experimental import pallas as pl
from jax.experimental.pallas import tpu as pltpu
from jax.sharding import PartitionSpec as P

BF = jnp.bfloat16
F32 = jnp.float32
SIDE = 4
SLOTS = 8
ROWS = 32
MINE = 4
FETCH_ORDER = (0, 1, 3, 2)
ANY = pl.BlockSpec(memory_space=pl.ANY)
WHOLE = pl.BlockSpec(memory_space=pltpu.VMEM)
SCALARS = pl.BlockSpec(memory_space=pltpu.SMEM)
SMALL = pltpu.CompilerParams(vmem_limit_bytes=8 * 1024 * 1024)
ORDER = pltpu.CompilerParams(vmem_limit_bytes=12 * 1024 * 1024)
LIMIT = pltpu.CompilerParams(vmem_limit_bytes=60 * 1024 * 1024)
Z_GROUPS = [[z * SIDE + y for z in range(SIDE)] for y in range(SIDE)]
Y_GROUPS = [[z * SIDE + y for y in range(SIDE)] for z in range(SIDE)]


def dot(a, b):
    return jnp.dot(a, b, preferred_element_type=F32)


def dot_nt(a, b):
    return lax.dot_general(a, b, (((1,), (1,)), ((), ())), preferred_element_type=F32)


def dot_tn(a, b):
    return lax.dot_general(a, b, (((0,), (0,)), ((), ())), preferred_element_type=F32)


def along_x(block, distance):
    return lax.ppermute(block, "mp", [(i, (i + distance) % SIDE) for i in range(SIDE)])


def along_z(block, distance):
    pairs = [
        (z * SIDE + y, (z + distance) % SIDE * SIDE + y) for z in range(SIDE) for y in range(SIDE)
    ]
    return lax.ppermute(block, "dp", pairs)


def along_y(block, distance):
    pairs = [
        (z * SIDE + y, z * SIDE + (y + distance) % SIDE) for z in range(SIDE) for y in range(SIDE)
    ]
    return lax.ppermute(block, "dp", pairs)


def along_mine(block, distance):
    pairs = []
    for z in range(SIDE):
        for y in range(SIDE):
            here = z * SIDE + y
            pairs.append((here, (z + distance) % SIDE * SIDE + y))
            pairs.append((16 + here, 16 + z * SIDE + (y + distance) % SIDE))
    return lax.ppermute(block, ("segment", "dp"), pairs)


def along_other(block, distance):
    pairs = []
    for z in range(SIDE):
        for y in range(SIDE):
            here = z * SIDE + y
            pairs.append((here, z * SIDE + (y + distance) % SIDE))
            pairs.append((16 + here, 16 + (z + distance) % SIDE * SIDE + y))
    return lax.ppermute(block, ("segment", "dp"), pairs)


def swap(block):
    return lax.ppermute(block, "segment", [(0, 1), (1, 0)])


def after(value, *others):
    return lax.optimization_barrier((value,) + others)[0]


def spread_kernel(routing, place, slots, out):
    core, replica = place[0], place[1]
    for group in range(16):
        slot = jnp.int32(0)
        for j in range(MINE):
            q = routing[(core * 16 + group) * MINE + j]
            slot = jnp.where(lax.shift_right_logical(q, 3) == replica, q & 7, slot)
        out[group] = slots[slot]


def spread(routing, place, slots):
    shape = (16,) + slots.shape[1:]
    return pl.pallas_call(
        spread_kernel,
        in_specs=[SCALARS, SCALARS, WHOLE],
        out_specs=WHOLE,
        out_shape=jax.ShapeDtypeStruct(shape, slots.dtype),
        compiler_params=LIMIT,
    )(routing, place, slots)


def merge_kernel(routing, counts, place, arrived, image, out, sems):
    first = (place[0] * 16 + place[1]) * MINE
    copies = []
    for j in range(MINE):
        replica = lax.shift_right_logical(routing[first + j], 3)
        copy = pltpu.make_async_copy(arrived.at[replica], out.at[j], sems.at[j])
        copy.start()
        copies.append(copy)
    row = lax.broadcasted_iota(jnp.int32, out.shape[1:], 0)
    for j in range(MINE):
        copies[j].wait()
        out[j] = jnp.where(row < counts[first + j], image[j], out[j])


def merge(routing, counts, place, arrived, image):
    columns = arrived.shape[2]
    return pl.pallas_call(
        merge_kernel,
        in_specs=[SCALARS] * 3 + [ANY, WHOLE],
        out_specs=WHOLE,
        scratch_shapes=[pltpu.SemaphoreType.DMA((MINE,))],
        out_shape=jax.ShapeDtypeStruct((MINE, ROWS, columns), arrived.dtype),
        compiler_params=LIMIT,
    )(routing, counts, place, arrived, image).reshape(MINE * ROWS, columns)


def pick_kernel(routing, place, arrived, out, sems):
    first = (place[0] * 16 + place[1]) * MINE
    copies = []
    for j in range(MINE):
        replica = lax.shift_right_logical(routing[first + j], 3)
        copy = pltpu.make_async_copy(arrived.at[replica], out.at[j], sems.at[j])
        copy.start()
        copies.append(copy)
    for copy in copies:
        copy.wait()


def pick(routing, place, arrived):
    columns = arrived.shape[2]
    return pl.pallas_call(
        pick_kernel,
        in_specs=[SCALARS] * 2 + [ANY],
        out_specs=WHOLE,
        scratch_shapes=[pltpu.SemaphoreType.DMA((MINE,))],
        out_shape=jax.ShapeDtypeStruct((MINE, ROWS, columns), arrived.dtype),
        compiler_params=SMALL,
    )(routing, place, arrived).reshape(MINE * ROWS, columns)


def gelu_parts(x):
    scale = 0.7978845608028654
    t = jnp.tanh(scale * (x + 0.044715 * (x * x * x)))
    cdf = 0.5 * (1.0 + t)
    slope = cdf + 0.5 * x * (1.0 - t * t) * (scale * (1.0 + 3 * 0.044715 * (x * x)))
    return x * cdf, slope


def fetch_weights(section, place, own, other, held, sems):
    core, x = place[0], place[2]
    size = held.shape[1]

    def copy(source, d):
        start = pl.multiple_of(lax.rem(x - d + SIDE, SIDE) * size, size)
        return pltpu.make_async_copy(source.at[pl.ds(start, size)], held.at[d], sems.at[d])

    for d in FETCH_ORDER:

        @pl.when(core == section)
        def _():
            copy(own, d).start()

        @pl.when(core != section)
        def _():
            copy(other, d).start()

    return lambda d: copy(own, d).wait()


def forward_product(wait, held, blocks):
    total = None
    for d in FETCH_ORDER:
        wait(d)
        product = dot(blocks[d][...], held[d][...])
        total = product if total is None else total + product
    return total


def send_terms(local, held, put, first, wait=None):
    for d in (2, 1, 3, 0):
        block = (SIDE - d) % SIDE
        if wait is not None:
            wait(block)
        put(first + d, dot_nt(local, held[block][...]).astype(BF))


def forward_body(wait, held, blocks, put):
    activation, slope = gelu_parts(forward_product(wait, held, blocks))
    put(0, (blocks[0][...].astype(F32) + activation).astype(BF))
    put(1, slope)


def middle_body(wait, held, operands, put):
    _, slope = gelu_parts(forward_product(wait, held, operands[:SIDE]))
    local = (slope * operands[SIDE][...].astype(F32)).astype(BF)
    put(0, local)
    send_terms(local, held, put, 1)


def summed(cotangent, terms):
    total = terms[0][...].astype(F32)
    for term in terms[1:]:
        total = total + term[...].astype(F32)
    return (cotangent[...].astype(F32) + total).astype(BF)


def backward_body(wait, held, operands, put):
    upstream, slope, local1, place = operands[SIDE:]
    now = summed(upstream, operands[:SIDE])
    put(0, now)
    local = (slope[...] * now.astype(F32)).astype(BF)
    first = place[0] == 0
    put(1, jnp.where(first, local, local1[...]))
    put(2, jnp.where(first, local1[...], local))
    send_terms(local, held, put, 3, wait)


def step_kernel(body, section, count, outs, place, own, other, *refs):
    sources, targets = refs[:count], refs[count : count + outs]
    operands = refs[count + outs : 2 * count + outs]
    results = refs[2 * count + outs : 2 * (count + outs)]
    held, weight_sems, in_sems, out_sems = refs[2 * (count + outs) :]
    copies = [
        pltpu.make_async_copy(sources[n], operands[n], in_sems.at[n]) for n in range(count)
    ]
    for copy in copies:
        copy.start()
    wait = fetch_weights(section, place, own, other, held, weight_sems)
    for copy in copies:
        copy.wait()
    out_copies = []

    def put(n, value):
        results[n][...] = value
        copy = pltpu.make_async_copy(results[n], targets[n], out_sems.at[n])
        copy.start()
        out_copies.append(copy)

    body(wait, held, operands, put)
    for copy in out_copies:
        copy.wait()


def step(body, section, place, own, other, operands, outs):
    rows, columns = own.shape
    count = len(operands)
    return pl.pallas_call(
        functools.partial(step_kernel, body, section, count, len(outs)),
        in_specs=[SCALARS] + [ANY] * (2 + count),
        out_specs=[ANY] * len(outs),
        out_shape=outs,
        scratch_shapes=[
            *(pltpu.VMEM(value.shape, value.dtype) for value in list(operands) + list(outs)),
            pltpu.VMEM((SIDE, rows // SIDE, columns), own.dtype),
            pltpu.SemaphoreType.DMA((SIDE,)),
            pltpu.SemaphoreType.DMA((count,)),
            pltpu.SemaphoreType.DMA((len(outs),)),
        ],
        compiler_params=LIMIT,
    )(place, own, other, *operands)


def turn_kernel(place, own, other, *outs_and_sems):
    outs, sems = outs_and_sems[:-1], outs_and_sems[-1]
    core, x = place[0], place[2]
    size = outs[0].shape[0]

    def copy(source, n):
        block = lax.rem(x - n % SIDE + SIDE, SIDE)
        start = pl.multiple_of(block * size, size)
        return pltpu.make_async_copy(source.at[pl.ds(start, size)], outs[n], sems.at[n])

    for n in range(2 * SIDE):

        @pl.when(core == n // SIDE)
        def _():
            copy(own, n).start()

        @pl.when(core != n // SIDE)
        def _():
            copy(other, n).start()

    for n in range(2 * SIDE):
        copy(own, n).wait()


def turn(place, own, other):
    rows, columns = own.shape
    blocks = pl.pallas_call(
        turn_kernel,
        in_specs=[pl.BlockSpec(memory_space=pltpu.SMEM), ANY, ANY],
        out_specs=[pl.BlockSpec(memory_space=pltpu.VMEM)] * (2 * SIDE),
        scratch_shapes=[pltpu.SemaphoreType.DMA((2 * SIDE,))],
        out_shape=[pltpu.VMEM((rows // SIDE, columns), own.dtype)] * (2 * SIDE),
        compiler_params=SMALL,
    )(place, own, other)
    return (blocks[:SIDE], blocks[SIDE:])


def held_kernel(body, count, outs, *refs):
    weights, operands, results = refs[:SIDE], refs[SIDE : SIDE + count], refs[SIDE + count :]

    def put(n, value):
        results[n][...] = value

    body(lambda d: None, weights, operands, put)


def held_step(body, weights, operands, outs):
    count = len(operands)
    return pl.pallas_call(
        functools.partial(held_kernel, body, count, len(outs)),
        in_specs=[
            SCALARS if value.dtype == jnp.int32 else WHOLE for value in list(weights) + operands
        ],
        out_specs=[WHOLE] * len(outs),
        out_shape=outs,
        compiler_params=pltpu.CompilerParams(vmem_limit_bytes=16 * 1024 * 1024),
    )(*weights, *operands)


def last_kernel(counts, place, r0, r1, r2, r3, cotangent, out):
    now = summed(cotangent, (r0, r1, r2, r3))
    first = (place[0] * 16 + place[1]) * MINE
    row = lax.broadcasted_iota(jnp.int32, (ROWS, now.shape[1]), 0)
    for j in range(MINE):
        rows = pl.ds(j * ROWS, ROWS)
        held = now[j * ROWS : (j + 1) * ROWS]
        out[rows] = jnp.where(row < counts[first + j], held, jnp.zeros_like(held))


def weight_grad_kernel(place, *refs):
    rows, local, outs, held = refs[:4], refs[4:8], refs[8:12], refs[12]
    there = jnp.where(place[0] == 0, place[3], place[4])
    total = None
    for n in range(SIDE):
        product = dot_tn(rows[n][...], local[n][...])
        total = product if total is None else total + product
    held[...] = total
    size = outs[0].shape[0]
    for j in range(SIDE):
        start = pl.multiple_of(lax.rem(there + j, SIDE) * size, size)
        outs[j][...] = held[pl.ds(start, size)].astype(BF)


def weight_grad(place, rows, local):
    columns = local[0].shape[1]
    shape = jax.ShapeDtypeStruct((columns // SIDE, columns), BF)
    return pl.pallas_call(
        weight_grad_kernel,
        in_specs=[SCALARS] + [WHOLE] * (2 * SIDE),
        out_specs=[WHOLE] * SIDE,
        out_shape=[shape] * SIDE,
        scratch_shapes=[pltpu.VMEM((columns, columns), F32)],
        compiler_params=LIMIT,
    )(place, *rows, *local)


def columns_kernel(place, activated, far, *outs):
    core, y, z = place[0], place[3], place[4]
    half, tokens = far.shape
    rows = half // SIDE
    part = rows // SIDE

    def put(out, to, start):
        out[to, :tokens] = activated[pl.ds(pl.multiple_of(core * half + start, part), to.size)]
        out[to, tokens:] = far[pl.ds(pl.multiple_of(start, part), to.size)]

    @pl.when(core == 0)
    def _():
        for e, out in enumerate(outs):
            put(out, pl.ds(0, rows), lax.rem(z + e, SIDE) * rows)

    @pl.when(core == 1)
    def _():
        for e, out in enumerate(outs):
            for m in range(SIDE):
                put(out, pl.ds(m * part, part), m * rows + lax.rem(y + e, SIDE) * part)


def columns_out(place, activated, far):
    half, tokens = far.shape
    shape = jax.ShapeDtypeStruct((half // SIDE, 2 * tokens), BF)
    return pl.pallas_call(
        columns_kernel,
        in_specs=[SCALARS] + [WHOLE] * 2,
        out_specs=[WHOLE] * SIDE,
        out_shape=[shape] * SIDE,
        compiler_params=ORDER,
    )(place, activated, far)


def merger_kernel(place, *refs):
    acts, grads, outs, held = refs[:4], refs[4:8], refs[8:12], refs[12]
    there = jnp.where(place[0] == 0, place[3], place[4])
    total = None
    for n in range(SIDE):
        product = dot(acts[n][...], grads[n][...])
        total = product if total is None else total + product
    held[...] = total
    size = outs[0].shape[0]
    for j in range(SIDE):
        start = pl.multiple_of(lax.rem(there + j, SIDE) * size, size)
        outs[j][...] = held[pl.ds(start, size)].astype(BF)


def merger_parts(place, acts, grads):
    columns = grads[0].shape[1]
    rows = acts[0].shape[0]
    shape = jax.ShapeDtypeStruct((rows // SIDE, columns), BF)
    return pl.pallas_call(
        merger_kernel,
        in_specs=[SCALARS] + [WHOLE] * (2 * SIDE),
        out_specs=[WHOLE] * SIDE,
        out_shape=[shape] * SIDE,
        scratch_shapes=[pltpu.VMEM((rows, columns), F32)],
        compiler_params=LIMIT,
    )(place, *acts, *grads)


def order_kernel(place, *refs):
    blocks, keep, give = refs[: 2 * SIDE], refs[2 * SIDE], refs[2 * SIDE + 1]
    core, x, y, z = place[0], place[2], place[3], place[4]
    part = blocks[0].shape[1] // SIDE

    def write(section, out):
        for d in range(SIDE):
            block = blocks[section * SIDE + d]
            if section == 0:
                out[lax.rem(x - d - z + 2 * SIDE, SIDE)] = block[...]
            else:
                to = pl.ds(pl.multiple_of(lax.rem(x - d + SIDE, SIDE) * part, part), part)
                for e in range(SIDE):
                    of = pl.ds(pl.multiple_of(lax.rem(y + e, SIDE) * part, part), part)
                    out[e, :, to] = block[:, of]

    @pl.when(core == 0)
    def _():
        write(0, keep)
        write(1, give)

    @pl.when(core == 1)
    def _():
        write(1, keep)
        write(0, give)


def order(place, blocks):
    shape = jax.ShapeDtypeStruct((SIDE,) + blocks[0].shape, BF)
    return pl.pallas_call(
        order_kernel,
        in_specs=[SCALARS] + [WHOLE] * (2 * SIDE),
        out_specs=[WHOLE] * 2,
        out_shape=[shape] * 2,
        compiler_params=ORDER,
    )(place, *blocks)


def pair_kernel(keep, far, out):
    rows = keep.shape[-2]
    out[..., pl.ds(0, rows), :] = keep[...]
    out[..., pl.ds(rows, rows), :] = far[...]


def pair(keep, far):
    shape = keep.shape[:-2] + (2 * keep.shape[-2], keep.shape[-1])
    return pl.pallas_call(
        pair_kernel,
        in_specs=[WHOLE] * 2,
        out_specs=WHOLE,
        out_shape=jax.ShapeDtypeStruct(shape, BF),
        compiler_params=ORDER,
    )(keep, far)


def pairs_kernel(keep, far, *outs):
    rows = keep.shape[1]
    for n, out in enumerate(outs):
        out[pl.ds(0, rows)] = keep[n]
        out[pl.ds(rows, rows)] = far[n]


def pairs(keep, far):
    count, rows, columns = keep.shape
    return pl.pallas_call(
        pairs_kernel,
        in_specs=[WHOLE] * 2,
        out_specs=[WHOLE] * count,
        out_shape=[jax.ShapeDtypeStruct((2 * rows, columns), BF)] * count,
        compiler_params=ORDER,
    )(keep, far)


def on_device(patches, merger_weight, image_counts, routing, text_embed, llm_weight, upstream):
    core = lax.axis_index("segment")
    x = lax.axis_index("mp")
    replica = lax.axis_index("dp")
    z, y = replica // SIDE, replica % SIDE
    place = jnp.stack([core, replica, x, y, z]).astype(jnp.int32)
    columns = merger_weight.shape[1]
    merger = patches.shape[2]
    tokens = MINE * ROWS
    block = jax.ShapeDtypeStruct((tokens, columns), BF)

    own = llm_weight[0]
    other = swap(own)
    send_text = spread(routing, place, text_embed.reshape(SLOTS, ROWS, columns))
    arrived_text = lax.all_to_all(send_text, "dp", 0, 0, tiled=True)
    activated = jax.nn.gelu(patches.astype(F32)).astype(BF).reshape(tokens, merger)
    embeds = dot(activated, merger_weight).astype(BF).reshape(MINE, ROWS, columns)
    send_ups = spread(routing, place, upstream.reshape(SLOTS, ROWS, columns))
    act_columns = activated.T
    act_far = swap(
        lax.dynamic_slice_in_dim(act_columns, (1 - core) * (merger // 2), merger // 2)
    )
    acts = columns_out(place, act_columns, act_far)
    acts = [acts[0]] + [along_mine(acts[e], e) for e in (1, 2, 3)]
    mine = [[c * 16 + n for n in g] for c, gs in ((0, Z_GROUPS), (1, Y_GROUPS)) for g in gs]
    arrived_text, embeds, acts, send_ups, other = lax.optimization_barrier(
        (arrived_text, embeds, acts, send_ups, other)
    )
    start = merge(routing, image_counts, place, arrived_text, embeds)

    blocks0 = [start] + [along_x(start, d) for d in (1, 2, 3)]
    arrived_ups = lax.all_to_all(after(send_ups, start), "dp", 0, 0, tiled=True)
    hidden, slope = step(
        forward_body, 0, place, own, other, blocks0, [block, jax.ShapeDtypeStruct(block.shape, F32)]
    )

    blocks1 = [hidden] + [along_x(hidden, d) for d in (1, 2, 3)]
    top = pick(routing, place, arrived_ups)
    weights = turn(place, own, after(other, top))
    local1, *terms = held_step(middle_body, weights[1], blocks1 + [top], [block] * 5)

    terms = [terms[0]] + [along_x(terms[d], d) for d in (1, 2, 3)]
    keep, give = order(place, [after(blocks0[0], local1)] + blocks0[1:] + blocks1)
    rows = pairs(keep, swap(give))
    rows = [rows[0]] + [along_mine(rows[e], e) for e in (1, 2, 3)]
    cotangent, keep, give, *sends = held_step(
        backward_body, weights[0], terms + [after(top, rows[0]), slope, local1, place], [block] * 7
    )

    ends = [sends[0]] + [along_x(sends[d], d) for d in (1, 2, 3)]
    local = pair(keep, swap(give))
    local = [local] + [along_mine(local, e) for e in (1, 2, 3)]
    grad = pl.pallas_call(
        last_kernel,
        in_specs=[SCALARS, SCALARS] + [WHOLE] * 5,
        out_specs=WHOLE,
        out_shape=block,
        compiler_params=SMALL,
    )(image_counts, place, *ends, after(cotangent, *rows[1:]))
    grad = pair(grad, swap(grad))
    going = grad
    grads = [grad] + [along_mine(going, e) for e in (1, 2, 3)]

    parts = weight_grad(place, [after(rows[0], grad)] + rows[1:], local)
    llm_grad = parts[0].astype(F32)
    for j in (1, 2, 3):
        llm_grad = llm_grad + along_other(parts[j], j).astype(F32)
    llm_grad = llm_grad[None]

    parts = merger_parts(place, [acts[0]] + acts[1:], grads)
    merger_grad = parts[0].astype(F32)
    for j in (1, 2, 3):
        merger_grad = merger_grad + along_other(parts[j], j).astype(F32)
    return (llm_grad, merger_grad)


def solution(mesh):
    return jax.shard_map(
        on_device,
        mesh=mesh,
        in_specs=(
            P(("segment", "dp"), None, None),
            P(None, "mp"),
            P(),
            P(),
            P(None, "dp", "mp"),
            P("segment", None, "mp"),
            P(None, "dp", "mp"),
        ),
        out_specs=(P("segment", "dp", "mp"), P(("segment", "dp"), "mp")),
        check_vma=False,
    )
```

```python
import functools

import jax
import jax.numpy as jnp
from jax import lax
from jax.experimental import pallas as pl
from jax.experimental.pallas import tpu as pltpu
from jax.sharding import PartitionSpec as P

BF = jnp.bfloat16
F32 = jnp.float32
SIDE = 4
SLOTS = 8
ROWS = 32
MINE = 4
FETCH_ORDER = (0, 1, 3, 2)
ANY = pl.BlockSpec(memory_space=pl.ANY)
WHOLE = pl.BlockSpec(memory_space=pltpu.VMEM)
SCALARS = pl.BlockSpec(memory_space=pltpu.SMEM)
SMALL = pltpu.CompilerParams(vmem_limit_bytes=8 * 1024 * 1024)
ORDER = pltpu.CompilerParams(vmem_limit_bytes=12 * 1024 * 1024)
LIMIT = pltpu.CompilerParams(vmem_limit_bytes=60 * 1024 * 1024)
Z_GROUPS = [[z * SIDE + y for z in range(SIDE)] for y in range(SIDE)]
Y_GROUPS = [[z * SIDE + y for y in range(SIDE)] for z in range(SIDE)]


def dot(a, b):
    return jnp.dot(a, b, preferred_element_type=F32)


def dot_nt(a, b):
    return lax.dot_general(a, b, (((1,), (1,)), ((), ())), preferred_element_type=F32)


def dot_tn(a, b):
    return lax.dot_general(a, b, (((0,), (0,)), ((), ())), preferred_element_type=F32)


def along_x(block, distance):
    return lax.ppermute(block, "mp", [(i, (i + distance) % SIDE) for i in range(SIDE)])


def along_z(block, distance):
    pairs = [
        (z * SIDE + y, (z + distance) % SIDE * SIDE + y) for z in range(SIDE) for y in range(SIDE)
    ]
    return lax.ppermute(block, "dp", pairs)


def along_y(block, distance):
    pairs = [
        (z * SIDE + y, z * SIDE + (y + distance) % SIDE) for z in range(SIDE) for y in range(SIDE)
    ]
    return lax.ppermute(block, "dp", pairs)


def along_mine(block, distance):
    pairs = []
    for z in range(SIDE):
        for y in range(SIDE):
            here = z * SIDE + y
            pairs.append((here, (z + distance) % SIDE * SIDE + y))
            pairs.append((16 + here, 16 + z * SIDE + (y + distance) % SIDE))
    return lax.ppermute(block, ("segment", "dp"), pairs)


def along_other(block, distance):
    pairs = []
    for z in range(SIDE):
        for y in range(SIDE):
            here = z * SIDE + y
            pairs.append((here, z * SIDE + (y + distance) % SIDE))
            pairs.append((16 + here, 16 + (z + distance) % SIDE * SIDE + y))
    return lax.ppermute(block, ("segment", "dp"), pairs)


def swap(block):
    return lax.ppermute(block, "segment", [(0, 1), (1, 0)])


def after(value, *others):
    return lax.optimization_barrier((value,) + others)[0]


def spread_kernel(routing, place, slots, out):
    core, replica = place[0], place[1]
    for group in range(16):
        slot = jnp.int32(0)
        for j in range(MINE):
            q = routing[(core * 16 + group) * MINE + j]
            slot = jnp.where(lax.shift_right_logical(q, 3) == replica, q & 7, slot)
        out[group] = slots[slot]


def spread(routing, place, slots):
    shape = (16,) + slots.shape[1:]
    return pl.pallas_call(
        spread_kernel,
        in_specs=[SCALARS, SCALARS, WHOLE],
        out_specs=WHOLE,
        out_shape=jax.ShapeDtypeStruct(shape, slots.dtype),
        compiler_params=LIMIT,
    )(routing, place, slots)


def merge_kernel(routing, counts, place, arrived, image, out, sems):
    first = (place[0] * 16 + place[1]) * MINE
    copies = []
    for j in range(MINE):
        replica = lax.shift_right_logical(routing[first + j], 3)
        copy = pltpu.make_async_copy(arrived.at[replica], out.at[j], sems.at[j])
        copy.start()
        copies.append(copy)
    row = lax.broadcasted_iota(jnp.int32, out.shape[1:], 0)
    for j in range(MINE):
        copies[j].wait()
        out[j] = jnp.where(row < counts[first + j], image[j], out[j])


def merge(routing, counts, place, arrived, image):
    columns = arrived.shape[2]
    return pl.pallas_call(
        merge_kernel,
        in_specs=[SCALARS] * 3 + [ANY, WHOLE],
        out_specs=WHOLE,
        scratch_shapes=[pltpu.SemaphoreType.DMA((MINE,))],
        out_shape=jax.ShapeDtypeStruct((MINE, ROWS, columns), arrived.dtype),
        compiler_params=LIMIT,
    )(routing, counts, place, arrived, image).reshape(MINE * ROWS, columns)


def pick_kernel(routing, place, arrived, out, sems):
    first = (place[0] * 16 + place[1]) * MINE
    copies = []
    for j in range(MINE):
        replica = lax.shift_right_logical(routing[first + j], 3)
        copy = pltpu.make_async_copy(arrived.at[replica], out.at[j], sems.at[j])
        copy.start()
        copies.append(copy)
    for copy in copies:
        copy.wait()


def pick(routing, place, arrived):
    columns = arrived.shape[2]
    return pl.pallas_call(
        pick_kernel,
        in_specs=[SCALARS] * 2 + [ANY],
        out_specs=WHOLE,
        scratch_shapes=[pltpu.SemaphoreType.DMA((MINE,))],
        out_shape=jax.ShapeDtypeStruct((MINE, ROWS, columns), arrived.dtype),
        compiler_params=SMALL,
    )(routing, place, arrived).reshape(MINE * ROWS, columns)


def gelu_parts(x):
    scale = 0.7978845608028654
    t = jnp.tanh(scale * (x + 0.044715 * (x * x * x)))
    cdf = 0.5 * (1.0 + t)
    slope = cdf + 0.5 * x * (1.0 - t * t) * (scale * (1.0 + 3 * 0.044715 * (x * x)))
    return x * cdf, slope


def fetch_weights(section, place, own, other, held, sems):
    core, x = place[0], place[2]
    size = held.shape[1]

    def copy(source, d):
        start = pl.multiple_of(lax.rem(x - d + SIDE, SIDE) * size, size)
        return pltpu.make_async_copy(source.at[pl.ds(start, size)], held.at[d], sems.at[d])

    for d in FETCH_ORDER:

        @pl.when(core == section)
        def _():
            copy(own, d).start()

        @pl.when(core != section)
        def _():
            copy(other, d).start()

    return lambda d: copy(own, d).wait()


def forward_product(wait, held, blocks):
    total = None
    for d in FETCH_ORDER:
        wait(d)
        product = dot(blocks[d][...], held[d][...])
        total = product if total is None else total + product
    return total


def send_terms(local, held, put, first, wait=None):
    for d in (2, 1, 3, 0):
        block = (SIDE - d) % SIDE
        if wait is not None:
            wait(block)
        put(first + d, dot_nt(local, held[block][...]).astype(BF))


def forward_body(wait, held, blocks, put):
    activation, slope = gelu_parts(forward_product(wait, held, blocks))
    put(0, (blocks[0][...].astype(F32) + activation).astype(BF))
    put(1, slope)


def middle_body(wait, held, operands, put):
    _, slope = gelu_parts(forward_product(wait, held, operands[:SIDE]))
    local = (slope * operands[SIDE][...].astype(F32)).astype(BF)
    put(0, local)
    send_terms(local, held, put, 1)


def summed(cotangent, terms):
    total = terms[0][...].astype(F32)
    for term in terms[1:]:
        total = total + term[...].astype(F32)
    return (cotangent[...].astype(F32) + total).astype(BF)


def backward_body(wait, held, operands, put):
    upstream, slope, local1, place = operands[SIDE:]
    now = summed(upstream, operands[:SIDE])
    put(0, now)
    local = (slope[...] * now.astype(F32)).astype(BF)
    first = place[0] == 0
    put(1, jnp.where(first, local, local1[...]))
    put(2, jnp.where(first, local1[...], local))
    send_terms(local, held, put, 3, wait)


def step_kernel(body, section, count, outs, place, own, other, *refs):
    sources, targets = refs[:count], refs[count : count + outs]
    operands = refs[count + outs : 2 * count + outs]
    results = refs[2 * count + outs : 2 * (count + outs)]
    held, weight_sems, in_sems, out_sems = refs[2 * (count + outs) :]
    copies = [
        pltpu.make_async_copy(sources[n], operands[n], in_sems.at[n]) for n in range(count)
    ]
    for copy in copies:
        copy.start()
    wait = fetch_weights(section, place, own, other, held, weight_sems)
    for copy in copies:
        copy.wait()
    out_copies = []

    def put(n, value):
        results[n][...] = value
        copy = pltpu.make_async_copy(results[n], targets[n], out_sems.at[n])
        copy.start()
        out_copies.append(copy)

    body(wait, held, operands, put)
    for copy in out_copies:
        copy.wait()


def step(body, section, place, own, other, operands, outs):
    rows, columns = own.shape
    count = len(operands)
    return pl.pallas_call(
        functools.partial(step_kernel, body, section, count, len(outs)),
        in_specs=[SCALARS] + [ANY] * (2 + count),
        out_specs=[ANY] * len(outs),
        out_shape=outs,
        scratch_shapes=[
            *(pltpu.VMEM(value.shape, value.dtype) for value in list(operands) + list(outs)),
            pltpu.VMEM((SIDE, rows // SIDE, columns), own.dtype),
            pltpu.SemaphoreType.DMA((SIDE,)),
            pltpu.SemaphoreType.DMA((count,)),
            pltpu.SemaphoreType.DMA((len(outs),)),
        ],
        compiler_params=LIMIT,
    )(place, own, other, *operands)


def turn_kernel(place, own, other, *outs_and_sems):
    outs, sems = outs_and_sems[:-1], outs_and_sems[-1]
    core, x = place[0], place[2]
    size = outs[0].shape[0]

    def copy(source, n):
        block = lax.rem(x - n % SIDE + SIDE, SIDE)
        start = pl.multiple_of(block * size, size)
        return pltpu.make_async_copy(source.at[pl.ds(start, size)], outs[n], sems.at[n])

    for n in range(2 * SIDE):

        @pl.when(core == n // SIDE)
        def _():
            copy(own, n).start()

        @pl.when(core != n // SIDE)
        def _():
            copy(other, n).start()

    for n in range(2 * SIDE):
        copy(own, n).wait()


def turn(place, own, other):
    rows, columns = own.shape
    blocks = pl.pallas_call(
        turn_kernel,
        in_specs=[pl.BlockSpec(memory_space=pltpu.SMEM), ANY, ANY],
        out_specs=[pl.BlockSpec(memory_space=pltpu.VMEM)] * (2 * SIDE),
        scratch_shapes=[pltpu.SemaphoreType.DMA((2 * SIDE,))],
        out_shape=[pltpu.VMEM((rows // SIDE, columns), own.dtype)] * (2 * SIDE),
        compiler_params=SMALL,
    )(place, own, other)
    return (blocks[:SIDE], blocks[SIDE:])


def held_kernel(body, count, outs, *refs):
    weights, operands, results = refs[:SIDE], refs[SIDE : SIDE + count], refs[SIDE + count :]

    def put(n, value):
        results[n][...] = value

    body(lambda d: None, weights, operands, put)


def held_step(body, weights, operands, outs):
    count = len(operands)
    return pl.pallas_call(
        functools.partial(held_kernel, body, count, len(outs)),
        in_specs=[
            SCALARS if value.dtype == jnp.int32 else WHOLE for value in list(weights) + operands
        ],
        out_specs=[WHOLE] * len(outs),
        out_shape=outs,
        compiler_params=pltpu.CompilerParams(vmem_limit_bytes=16 * 1024 * 1024),
    )(*weights, *operands)


def last_kernel(counts, place, r0, r1, r2, r3, cotangent, out):
    now = summed(cotangent, (r0, r1, r2, r3))
    first = (place[0] * 16 + place[1]) * MINE
    row = lax.broadcasted_iota(jnp.int32, (ROWS, now.shape[1]), 0)
    for j in range(MINE):
        rows = pl.ds(j * ROWS, ROWS)
        held = now[j * ROWS : (j + 1) * ROWS]
        out[rows] = jnp.where(row < counts[first + j], held, jnp.zeros_like(held))


def weight_grad_kernel(place, *refs):
    rows, local, outs, held = refs[:4], refs[4:8], refs[8:12], refs[12]
    there = jnp.where(place[0] == 0, place[3], place[4])
    total = None
    for n in range(SIDE):
        product = dot_tn(rows[n][...], local[n][...])
        total = product if total is None else total + product
    held[...] = total
    size = outs[0].shape[0]
    for j in range(SIDE):
        start = pl.multiple_of(lax.rem(there + j, SIDE) * size, size)
        outs[j][...] = held[pl.ds(start, size)].astype(BF)


def weight_grad(place, rows, local):
    columns = local[0].shape[1]
    shape = jax.ShapeDtypeStruct((columns // SIDE, columns), BF)
    return pl.pallas_call(
        weight_grad_kernel,
        in_specs=[SCALARS] + [WHOLE] * (2 * SIDE),
        out_specs=[WHOLE] * SIDE,
        out_shape=[shape] * SIDE,
        scratch_shapes=[pltpu.VMEM((columns, columns), F32)],
        compiler_params=LIMIT,
    )(place, *rows, *local)


def columns_kernel(place, activated, far, *outs):
    core, y, z = place[0], place[3], place[4]
    half, tokens = far.shape
    rows = half // SIDE
    part = rows // SIDE

    def put(out, to, start):
        out[to, :tokens] = activated[pl.ds(pl.multiple_of(core * half + start, part), to.size)]
        out[to, tokens:] = far[pl.ds(pl.multiple_of(start, part), to.size)]

    @pl.when(core == 0)
    def _():
        for e, out in enumerate(outs):
            put(out, pl.ds(0, rows), lax.rem(z + e, SIDE) * rows)

    @pl.when(core == 1)
    def _():
        for e, out in enumerate(outs):
            for m in range(SIDE):
                put(out, pl.ds(m * part, part), m * rows + lax.rem(y + e, SIDE) * part)


def columns_out(place, activated, far):
    half, tokens = far.shape
    shape = jax.ShapeDtypeStruct((half // SIDE, 2 * tokens), BF)
    return pl.pallas_call(
        columns_kernel,
        in_specs=[SCALARS] + [WHOLE] * 2,
        out_specs=[WHOLE] * SIDE,
        out_shape=[shape] * SIDE,
        compiler_params=ORDER,
    )(place, activated, far)


def merger_kernel(place, *refs):
    acts, grads, outs, held = refs[:4], refs[4:8], refs[8:12], refs[12]
    there = jnp.where(place[0] == 0, place[3], place[4])
    total = None
    for n in range(SIDE):
        product = dot(acts[n][...], grads[n][...])
        total = product if total is None else total + product
    held[...] = total
    size = outs[0].shape[0]
    for j in range(SIDE):
        start = pl.multiple_of(lax.rem(there + j, SIDE) * size, size)
        outs[j][...] = held[pl.ds(start, size)].astype(BF)


def merger_parts(place, acts, grads):
    columns = grads[0].shape[1]
    rows = acts[0].shape[0]
    shape = jax.ShapeDtypeStruct((rows // SIDE, columns), BF)
    return pl.pallas_call(
        merger_kernel,
        in_specs=[SCALARS] + [WHOLE] * (2 * SIDE),
        out_specs=[WHOLE] * SIDE,
        out_shape=[shape] * SIDE,
        scratch_shapes=[pltpu.VMEM((rows, columns), F32)],
        compiler_params=LIMIT,
    )(place, *acts, *grads)


def order_kernel(place, *refs):
    blocks, keep, give = refs[: 2 * SIDE], refs[2 * SIDE], refs[2 * SIDE + 1]
    core, x, y, z = place[0], place[2], place[3], place[4]
    part = blocks[0].shape[1] // SIDE

    def write(section, out):
        for d in range(SIDE):
            block = blocks[section * SIDE + d]
            if section == 0:
                out[lax.rem(x - d - z + 2 * SIDE, SIDE)] = block[...]
            else:
                to = pl.ds(pl.multiple_of(lax.rem(x - d + SIDE, SIDE) * part, part), part)
                for e in range(SIDE):
                    of = pl.ds(pl.multiple_of(lax.rem(y + e, SIDE) * part, part), part)
                    out[e, :, to] = block[:, of]

    @pl.when(core == 0)
    def _():
        write(0, keep)
        write(1, give)

    @pl.when(core == 1)
    def _():
        write(1, keep)
        write(0, give)


def order(place, blocks):
    shape = jax.ShapeDtypeStruct((SIDE,) + blocks[0].shape, BF)
    return pl.pallas_call(
        order_kernel,
        in_specs=[SCALARS] + [WHOLE] * (2 * SIDE),
        out_specs=[WHOLE] * 2,
        out_shape=[shape] * 2,
        compiler_params=ORDER,
    )(place, *blocks)


def pair_kernel(keep, far, out):
    rows = keep.shape[-2]
    out[..., pl.ds(0, rows), :] = keep[...]
    out[..., pl.ds(rows, rows), :] = far[...]


def pair(keep, far):
    shape = keep.shape[:-2] + (2 * keep.shape[-2], keep.shape[-1])
    return pl.pallas_call(
        pair_kernel,
        in_specs=[WHOLE] * 2,
        out_specs=WHOLE,
        out_shape=jax.ShapeDtypeStruct(shape, BF),
        compiler_params=ORDER,
    )(keep, far)


def pairs_kernel(keep, far, *outs):
    rows = keep.shape[1]
    for n, out in enumerate(outs):
        out[pl.ds(0, rows)] = keep[n]
        out[pl.ds(rows, rows)] = far[n]


def pairs(keep, far):
    count, rows, columns = keep.shape
    return pl.pallas_call(
        pairs_kernel,
        in_specs=[WHOLE] * 2,
        out_specs=[WHOLE] * count,
        out_shape=[jax.ShapeDtypeStruct((2 * rows, columns), BF)] * count,
        compiler_params=ORDER,
    )(keep, far)


def on_device(patches, merger_weight, image_counts, routing, text_embed, llm_weight, upstream):
    core = lax.axis_index("segment")
    x = lax.axis_index("mp")
    replica = lax.axis_index("dp")
    z, y = replica // SIDE, replica % SIDE
    place = jnp.stack([core, replica, x, y, z]).astype(jnp.int32)
    columns = merger_weight.shape[1]
    merger = patches.shape[2]
    tokens = MINE * ROWS
    block = jax.ShapeDtypeStruct((tokens, columns), BF)

    own = llm_weight[0]
    other = swap(own)
    send_text = spread(routing, place, text_embed.reshape(SLOTS, ROWS, columns))
    arrived_text = lax.all_to_all(send_text, "dp", 0, 0, tiled=True)
    activated = jax.nn.gelu(patches.astype(F32)).astype(BF).reshape(tokens, merger)
    embeds = dot(activated, merger_weight).astype(BF).reshape(MINE, ROWS, columns)
    send_ups = spread(routing, place, upstream.reshape(SLOTS, ROWS, columns))
    act_columns = activated.T
    act_far = swap(
        lax.dynamic_slice_in_dim(act_columns, (1 - core) * (merger // 2), merger // 2)
    )
    acts = columns_out(place, act_columns, act_far)
    acts = [acts[0]] + [along_mine(acts[e], e) for e in (1, 2, 3)]
    mine = [[c * 16 + n for n in g] for c, gs in ((0, Z_GROUPS), (1, Y_GROUPS)) for g in gs]
    arrived_text, embeds, acts, send_ups, other = lax.optimization_barrier(
        (arrived_text, embeds, acts, send_ups, other)
    )
    start = merge(routing, image_counts, place, arrived_text, embeds)

    blocks0 = [start] + [along_x(start, d) for d in (1, 2, 3)]
    arrived_ups = lax.all_to_all(after(send_ups, start), "dp", 0, 0, tiled=True)
    hidden, slope = step(
        forward_body, 0, place, own, other, blocks0, [block, jax.ShapeDtypeStruct(block.shape, F32)]
    )

    blocks1 = [hidden] + [along_x(hidden, d) for d in (1, 2, 3)]
    top = pick(routing, place, arrived_ups)
    weights = turn(place, own, after(other, top))
    local1, *terms = held_step(middle_body, weights[1], blocks1 + [top], [block] * 5)

    terms = [terms[0]] + [along_x(terms[d], d) for d in (1, 2, 3)]
    keep, give = order(place, [after(blocks0[0], local1)] + blocks0[1:] + blocks1)
    rows = pairs(keep, swap(give))
    rows = [rows[0]] + [along_mine(rows[e], e) for e in (1, 2, 3)]
    cotangent, keep, give, *sends = held_step(
        backward_body, weights[0], terms + [after(top, rows[0]), slope, local1, place], [block] * 7
    )

    ends = [sends[0]] + [along_x(sends[d], d) for d in (1, 2, 3)]
    local = pair(keep, swap(give))
    local = [local] + [along_mine(local, e) for e in (1, 2, 3)]
    grad = pl.pallas_call(
        last_kernel,
        in_specs=[SCALARS, SCALARS] + [WHOLE] * 5,
        out_specs=WHOLE,
        out_shape=block,
        compiler_params=SMALL,
    )(image_counts, place, *ends, after(cotangent, *rows[1:], local[0]))
    grad = pair(grad, swap(grad))
    going = after(grad, local[1], local[3])
    grads = [grad] + [along_mine(going, e) for e in (1, 2, 3)]

    parts = weight_grad(place, [after(rows[0], grad)] + rows[1:], local)
    llm_grad = parts[0].astype(F32)
    for j in (1, 2, 3):
        llm_grad = llm_grad + along_other(parts[j], j).astype(F32)
    llm_grad = llm_grad[None]

    parts = merger_parts(place, [acts[0]] + acts[1:], grads)
    merger_grad = parts[0].astype(F32)
    for j in (1, 2, 3):
        merger_grad = merger_grad + along_other(parts[j], j).astype(F32)
    return (llm_grad, merger_grad)


def solution(mesh):
    return jax.shard_map(
        on_device,
        mesh=mesh,
        in_specs=(
            P(("segment", "dp"), None, None),
            P(None, "mp"),
            P(),
            P(),
            P(None, "dp", "mp"),
            P("segment", None, "mp"),
            P(None, "dp", "mp"),
        ),
        out_specs=(P("segment", "dp", "mp"), P(("segment", "dp"), "mp")),
        check_vma=False,
    )
```

```python
import functools

import jax
import jax.numpy as jnp
from jax import lax
from jax.experimental import pallas as pl
from jax.experimental.pallas import tpu as pltpu
from jax.sharding import PartitionSpec as P

BF = jnp.bfloat16
F32 = jnp.float32
SIDE = 4
SLOTS = 8
ROWS = 32
MINE = 4
FETCH_ORDER = (0, 1, 3, 2)
ANY = pl.BlockSpec(memory_space=pl.ANY)
WHOLE = pl.BlockSpec(memory_space=pltpu.VMEM)
SCALARS = pl.BlockSpec(memory_space=pltpu.SMEM)
SMALL = pltpu.CompilerParams(vmem_limit_bytes=8 * 1024 * 1024)
ORDER = pltpu.CompilerParams(vmem_limit_bytes=12 * 1024 * 1024)
LIMIT = pltpu.CompilerParams(vmem_limit_bytes=60 * 1024 * 1024)
Z_GROUPS = [[z * SIDE + y for z in range(SIDE)] for y in range(SIDE)]
Y_GROUPS = [[z * SIDE + y for y in range(SIDE)] for z in range(SIDE)]


def dot(a, b):
    return jnp.dot(a, b, preferred_element_type=F32)


def dot_nt(a, b):
    return lax.dot_general(a, b, (((1,), (1,)), ((), ())), preferred_element_type=F32)


def dot_tn(a, b):
    return lax.dot_general(a, b, (((0,), (0,)), ((), ())), preferred_element_type=F32)


def along_x(block, distance):
    return lax.ppermute(block, "mp", [(i, (i + distance) % SIDE) for i in range(SIDE)])


def along_z(block, distance):
    pairs = [
        (z * SIDE + y, (z + distance) % SIDE * SIDE + y) for z in range(SIDE) for y in range(SIDE)
    ]
    return lax.ppermute(block, "dp", pairs)


def along_y(block, distance):
    pairs = [
        (z * SIDE + y, z * SIDE + (y + distance) % SIDE) for z in range(SIDE) for y in range(SIDE)
    ]
    return lax.ppermute(block, "dp", pairs)


def along_mine(block, distance):
    pairs = []
    for z in range(SIDE):
        for y in range(SIDE):
            here = z * SIDE + y
            pairs.append((here, (z + distance) % SIDE * SIDE + y))
            pairs.append((16 + here, 16 + z * SIDE + (y + distance) % SIDE))
    return lax.ppermute(block, ("segment", "dp"), pairs)


def along_other(block, distance):
    pairs = []
    for z in range(SIDE):
        for y in range(SIDE):
            here = z * SIDE + y
            pairs.append((here, z * SIDE + (y + distance) % SIDE))
            pairs.append((16 + here, 16 + (z + distance) % SIDE * SIDE + y))
    return lax.ppermute(block, ("segment", "dp"), pairs)


def swap(block):
    return lax.ppermute(block, "segment", [(0, 1), (1, 0)])


def after(value, *others):
    return lax.optimization_barrier((value,) + others)[0]


def spread_kernel(routing, place, slots, out):
    core, replica = place[0], place[1]
    for group in range(16):
        slot = jnp.int32(0)
        for j in range(MINE):
            q = routing[(core * 16 + group) * MINE + j]
            slot = jnp.where(lax.shift_right_logical(q, 3) == replica, q & 7, slot)
        out[group] = slots[slot]


def spread(routing, place, slots):
    shape = (16,) + slots.shape[1:]
    return pl.pallas_call(
        spread_kernel,
        in_specs=[SCALARS, SCALARS, WHOLE],
        out_specs=WHOLE,
        out_shape=jax.ShapeDtypeStruct(shape, slots.dtype),
        compiler_params=LIMIT,
    )(routing, place, slots)


def merge_kernel(routing, counts, place, arrived, image, out, sems):
    first = (place[0] * 16 + place[1]) * MINE
    copies = []
    for j in range(MINE):
        replica = lax.shift_right_logical(routing[first + j], 3)
        copy = pltpu.make_async_copy(arrived.at[replica], out.at[j], sems.at[j])
        copy.start()
        copies.append(copy)
    row = lax.broadcasted_iota(jnp.int32, out.shape[1:], 0)
    for j in range(MINE):
        copies[j].wait()
        out[j] = jnp.where(row < counts[first + j], image[j], out[j])


def merge(routing, counts, place, arrived, image):
    columns = arrived.shape[2]
    return pl.pallas_call(
        merge_kernel,
        in_specs=[SCALARS] * 3 + [ANY, WHOLE],
        out_specs=WHOLE,
        scratch_shapes=[pltpu.SemaphoreType.DMA((MINE,))],
        out_shape=jax.ShapeDtypeStruct((MINE, ROWS, columns), arrived.dtype),
        compiler_params=LIMIT,
    )(routing, counts, place, arrived, image).reshape(MINE * ROWS, columns)


def pick_kernel(routing, place, arrived, out, sems):
    first = (place[0] * 16 + place[1]) * MINE
    copies = []
    for j in range(MINE):
        replica = lax.shift_right_logical(routing[first + j], 3)
        copy = pltpu.make_async_copy(arrived.at[replica], out.at[j], sems.at[j])
        copy.start()
        copies.append(copy)
    for copy in copies:
        copy.wait()


def pick(routing, place, arrived):
    columns = arrived.shape[2]
    return pl.pallas_call(
        pick_kernel,
        in_specs=[SCALARS] * 2 + [ANY],
        out_specs=WHOLE,
        scratch_shapes=[pltpu.SemaphoreType.DMA((MINE,))],
        out_shape=jax.ShapeDtypeStruct((MINE, ROWS, columns), arrived.dtype),
        compiler_params=SMALL,
    )(routing, place, arrived).reshape(MINE * ROWS, columns)


def gelu_parts(x):
    scale = 0.7978845608028654
    t = jnp.tanh(scale * (x + 0.044715 * (x * x * x)))
    cdf = 0.5 * (1.0 + t)
    slope = cdf + 0.5 * x * (1.0 - t * t) * (scale * (1.0 + 3 * 0.044715 * (x * x)))
    return x * cdf, slope


def fetch_weights(section, place, own, other, held, sems):
    core, x = place[0], place[2]
    size = held.shape[1]

    def copy(source, d):
        start = pl.multiple_of(lax.rem(x - d + SIDE, SIDE) * size, size)
        return pltpu.make_async_copy(source.at[pl.ds(start, size)], held.at[d], sems.at[d])

    for d in FETCH_ORDER:

        @pl.when(core == section)
        def _():
            copy(own, d).start()

        @pl.when(core != section)
        def _():
            copy(other, d).start()

    return lambda d: copy(own, d).wait()


def forward_product(wait, held, blocks):
    total = None
    for d in FETCH_ORDER:
        wait(d)
        product = dot(blocks[d][...], held[d][...])
        total = product if total is None else total + product
    return total


def send_terms(local, held, put, first, wait=None):
    for d in (2, 1, 3, 0):
        block = (SIDE - d) % SIDE
        if wait is not None:
            wait(block)
        put(first + d, dot_nt(local, held[block][...]).astype(BF))


def forward_body(wait, held, blocks, put):
    activation, slope = gelu_parts(forward_product(wait, held, blocks))
    put(0, (blocks[0][...].astype(F32) + activation).astype(BF))
    put(1, slope)


def middle_body(wait, held, operands, put):
    _, slope = gelu_parts(forward_product(wait, held, operands[:SIDE]))
    local = (slope * operands[SIDE][...].astype(F32)).astype(BF)
    put(0, local)
    send_terms(local, held, put, 1)


def summed(cotangent, terms):
    total = terms[0][...].astype(F32)
    for term in terms[1:]:
        total = total + term[...].astype(F32)
    return (cotangent[...].astype(F32) + total).astype(BF)


def backward_body(wait, held, operands, put):
    upstream, slope, local1, place = operands[SIDE:]
    now = summed(upstream, operands[:SIDE])
    put(0, now)
    local = (slope[...] * now.astype(F32)).astype(BF)
    first = place[0] == 0
    put(1, jnp.where(first, local, local1[...]))
    put(2, jnp.where(first, local1[...], local))
    send_terms(local, held, put, 3, wait)


def step_kernel(body, section, count, outs, place, own, other, *refs):
    sources, targets = refs[:count], refs[count : count + outs]
    operands = refs[count + outs : 2 * count + outs]
    results = refs[2 * count + outs : 2 * (count + outs)]
    held, weight_sems, in_sems, out_sems = refs[2 * (count + outs) :]
    copies = [
        pltpu.make_async_copy(sources[n], operands[n], in_sems.at[n]) for n in range(count)
    ]
    for copy in copies:
        copy.start()
    wait = fetch_weights(section, place, own, other, held, weight_sems)
    for copy in copies:
        copy.wait()
    out_copies = []

    def put(n, value):
        results[n][...] = value
        copy = pltpu.make_async_copy(results[n], targets[n], out_sems.at[n])
        copy.start()
        out_copies.append(copy)

    body(wait, held, operands, put)
    for copy in out_copies:
        copy.wait()


def step(body, section, place, own, other, operands, outs):
    rows, columns = own.shape
    count = len(operands)
    return pl.pallas_call(
        functools.partial(step_kernel, body, section, count, len(outs)),
        in_specs=[SCALARS] + [ANY] * (2 + count),
        out_specs=[ANY] * len(outs),
        out_shape=outs,
        scratch_shapes=[
            *(pltpu.VMEM(value.shape, value.dtype) for value in list(operands) + list(outs)),
            pltpu.VMEM((SIDE, rows // SIDE, columns), own.dtype),
            pltpu.SemaphoreType.DMA((SIDE,)),
            pltpu.SemaphoreType.DMA((count,)),
            pltpu.SemaphoreType.DMA((len(outs),)),
        ],
        compiler_params=LIMIT,
    )(place, own, other, *operands)


def turn_kernel(place, own, other, *outs_and_sems):
    outs, sems = outs_and_sems[:-1], outs_and_sems[-1]
    core, x = place[0], place[2]
    size = outs[0].shape[0]

    def copy(source, n):
        block = lax.rem(x - n % SIDE + SIDE, SIDE)
        start = pl.multiple_of(block * size, size)
        return pltpu.make_async_copy(source.at[pl.ds(start, size)], outs[n], sems.at[n])

    for n in range(len(outs)):

        @pl.when(core == n // SIDE)
        def _():
            copy(own, n).start()

        @pl.when(core != n // SIDE)
        def _():
            copy(other, n).start()

    for n in range(len(outs)):
        copy(own, n).wait()


def turn(place, own, other, sections=2, limit=8):
    rows, columns = own.shape
    blocks = pl.pallas_call(
        turn_kernel,
        in_specs=[pl.BlockSpec(memory_space=pltpu.SMEM), ANY, ANY],
        out_specs=[pl.BlockSpec(memory_space=pltpu.VMEM)] * (sections * SIDE),
        scratch_shapes=[pltpu.SemaphoreType.DMA((sections * SIDE,))],
        out_shape=[pltpu.VMEM((rows // SIDE, columns), own.dtype)] * (sections * SIDE),
        compiler_params=pltpu.CompilerParams(vmem_limit_bytes=limit * 1024 * 1024),
    )(place, own, other)
    return (blocks[:SIDE], blocks[SIDE:])


def held_kernel(body, count, outs, *refs):
    weights, operands, results = refs[:SIDE], refs[SIDE : SIDE + count], refs[SIDE + count :]

    def put(n, value):
        results[n][...] = value

    body(lambda d: None, weights, operands, put)


def held_step(body, weights, operands, outs):
    count = len(operands)
    return pl.pallas_call(
        functools.partial(held_kernel, body, count, len(outs)),
        in_specs=[
            SCALARS if value.dtype == jnp.int32 else WHOLE for value in list(weights) + operands
        ],
        out_specs=[WHOLE] * len(outs),
        out_shape=outs,
        compiler_params=pltpu.CompilerParams(vmem_limit_bytes=16 * 1024 * 1024),
    )(*weights, *operands)


def last_kernel(counts, place, r0, r1, r2, r3, cotangent, out):
    now = summed(cotangent, (r0, r1, r2, r3))
    first = (place[0] * 16 + place[1]) * MINE
    row = lax.broadcasted_iota(jnp.int32, (ROWS, now.shape[1]), 0)
    for j in range(MINE):
        rows = pl.ds(j * ROWS, ROWS)
        held = now[j * ROWS : (j + 1) * ROWS]
        out[rows] = jnp.where(row < counts[first + j], held, jnp.zeros_like(held))


def weight_grad_kernel(place, *refs):
    rows, local, outs, held = refs[:4], refs[4:8], refs[8:12], refs[12]
    there = jnp.where(place[0] == 0, place[3], place[4])
    total = None
    for n in range(SIDE):
        product = dot_tn(rows[n][...], local[n][...])
        total = product if total is None else total + product
    held[...] = total
    size = outs[0].shape[0]
    for j in range(SIDE):
        start = pl.multiple_of(lax.rem(there + j, SIDE) * size, size)
        outs[j][...] = held[pl.ds(start, size)].astype(BF)


def weight_grad(place, rows, local):
    columns = local[0].shape[1]
    shape = jax.ShapeDtypeStruct((columns // SIDE, columns), BF)
    return pl.pallas_call(
        weight_grad_kernel,
        in_specs=[SCALARS] + [WHOLE] * (2 * SIDE),
        out_specs=[WHOLE] * SIDE,
        out_shape=[shape] * SIDE,
        scratch_shapes=[pltpu.VMEM((columns, columns), F32)],
        compiler_params=LIMIT,
    )(place, *rows, *local)


def columns_kernel(place, activated, far, *outs):
    core, y, z = place[0], place[3], place[4]
    half, tokens = far.shape
    rows = half // SIDE
    part = rows // SIDE

    def put(out, to, start):
        out[to, :tokens] = activated[pl.ds(pl.multiple_of(core * half + start, part), to.size)]
        out[to, tokens:] = far[pl.ds(pl.multiple_of(start, part), to.size)]

    @pl.when(core == 0)
    def _():
        for e, out in enumerate(outs):
            put(out, pl.ds(0, rows), lax.rem(z + e, SIDE) * rows)

    @pl.when(core == 1)
    def _():
        for e, out in enumerate(outs):
            for m in range(SIDE):
                put(out, pl.ds(m * part, part), m * rows + lax.rem(y + e, SIDE) * part)


def columns_out(place, activated, far):
    half, tokens = far.shape
    shape = jax.ShapeDtypeStruct((half // SIDE, 2 * tokens), BF)
    return pl.pallas_call(
        columns_kernel,
        in_specs=[SCALARS] + [WHOLE] * 2,
        out_specs=[WHOLE] * SIDE,
        out_shape=[shape] * SIDE,
        compiler_params=ORDER,
    )(place, activated, far)


def merger_kernel(place, *refs):
    acts, grads, outs, held = refs[:4], refs[4:8], refs[8:12], refs[12]
    there = jnp.where(place[0] == 0, place[3], place[4])
    total = None
    for n in range(SIDE):
        product = dot(acts[n][...], grads[n][...])
        total = product if total is None else total + product
    held[...] = total
    size = outs[0].shape[0]
    for j in range(SIDE):
        start = pl.multiple_of(lax.rem(there + j, SIDE) * size, size)
        outs[j][...] = held[pl.ds(start, size)].astype(BF)


def merger_parts(place, acts, grads):
    columns = grads[0].shape[1]
    rows = acts[0].shape[0]
    shape = jax.ShapeDtypeStruct((rows // SIDE, columns), BF)
    return pl.pallas_call(
        merger_kernel,
        in_specs=[SCALARS] + [WHOLE] * (2 * SIDE),
        out_specs=[WHOLE] * SIDE,
        out_shape=[shape] * SIDE,
        scratch_shapes=[pltpu.VMEM((rows, columns), F32)],
        compiler_params=LIMIT,
    )(place, *acts, *grads)


def order_kernel(place, *refs):
    blocks, keep, give = refs[: 2 * SIDE], refs[2 * SIDE], refs[2 * SIDE + 1]
    core, x, y, z = place[0], place[2], place[3], place[4]
    part = blocks[0].shape[1] // SIDE

    def write(section, out):
        for d in range(SIDE):
            block = blocks[section * SIDE + d]
            if section == 0:
                out[lax.rem(x - d - z + 2 * SIDE, SIDE)] = block[...]
            else:
                to = pl.ds(pl.multiple_of(lax.rem(x - d + SIDE, SIDE) * part, part), part)
                for e in range(SIDE):
                    of = pl.ds(pl.multiple_of(lax.rem(y + e, SIDE) * part, part), part)
                    out[e, :, to] = block[:, of]

    @pl.when(core == 0)
    def _():
        write(0, keep)
        write(1, give)

    @pl.when(core == 1)
    def _():
        write(1, keep)
        write(0, give)


def order(place, blocks):
    shape = jax.ShapeDtypeStruct((SIDE,) + blocks[0].shape, BF)
    return pl.pallas_call(
        order_kernel,
        in_specs=[SCALARS] + [WHOLE] * (2 * SIDE),
        out_specs=[WHOLE] * 2,
        out_shape=[shape] * 2,
        compiler_params=ORDER,
    )(place, *blocks)


def pair_kernel(keep, far, out):
    rows = keep.shape[-2]
    out[..., pl.ds(0, rows), :] = keep[...]
    out[..., pl.ds(rows, rows), :] = far[...]


def pair(keep, far):
    shape = keep.shape[:-2] + (2 * keep.shape[-2], keep.shape[-1])
    return pl.pallas_call(
        pair_kernel,
        in_specs=[WHOLE] * 2,
        out_specs=WHOLE,
        out_shape=jax.ShapeDtypeStruct(shape, BF),
        compiler_params=ORDER,
    )(keep, far)


def pairs_kernel(keep, far, *outs):
    rows = keep.shape[1]
    for n, out in enumerate(outs):
        out[pl.ds(0, rows)] = keep[n]
        out[pl.ds(rows, rows)] = far[n]


def pairs(keep, far):
    count, rows, columns = keep.shape
    return pl.pallas_call(
        pairs_kernel,
        in_specs=[WHOLE] * 2,
        out_specs=[WHOLE] * count,
        out_shape=[jax.ShapeDtypeStruct((2 * rows, columns), BF)] * count,
        compiler_params=ORDER,
    )(keep, far)


def on_device(patches, merger_weight, image_counts, routing, text_embed, llm_weight, upstream):
    core = lax.axis_index("segment")
    x = lax.axis_index("mp")
    replica = lax.axis_index("dp")
    z, y = replica // SIDE, replica % SIDE
    place = jnp.stack([core, replica, x, y, z]).astype(jnp.int32)
    columns = merger_weight.shape[1]
    merger = patches.shape[2]
    tokens = MINE * ROWS
    block = jax.ShapeDtypeStruct((tokens, columns), BF)

    own = llm_weight[0]
    other = swap(own)
    send_text = spread(routing, place, text_embed.reshape(SLOTS, ROWS, columns))
    arrived_text = lax.all_to_all(send_text, "dp", 0, 0, tiled=True)
    activated = jax.nn.gelu(patches.astype(F32)).astype(BF).reshape(tokens, merger)
    embeds = dot(activated, merger_weight).astype(BF).reshape(MINE, ROWS, columns)
    send_ups = spread(routing, place, upstream.reshape(SLOTS, ROWS, columns))
    act_columns = activated.T
    act_far = swap(
        lax.dynamic_slice_in_dim(act_columns, (1 - core) * (merger // 2), merger // 2)
    )
    acts = columns_out(place, act_columns, act_far)
    acts = [acts[0]] + [along_mine(acts[e], e) for e in (1, 2, 3)]
    mine = [[c * 16 + n for n in g] for c, gs in ((0, Z_GROUPS), (1, Y_GROUPS)) for g in gs]
    arrived_text, embeds, acts, send_ups, other = lax.optimization_barrier(
        (arrived_text, embeds, acts, send_ups, other)
    )
    start = merge(routing, image_counts, place, arrived_text, embeds)

    blocks0 = [start] + [along_x(start, d) for d in (1, 2, 3)]
    arrived_ups = lax.all_to_all(after(send_ups, start), "dp", 0, 0, tiled=True)
    first_weights, _ = turn(place, own, after(other, start), 1, 50)
    hidden, slope = held_step(
        forward_body, first_weights, blocks0, [block, jax.ShapeDtypeStruct(block.shape, F32)]
    )

    blocks1 = [hidden] + [along_x(hidden, d) for d in (1, 2, 3)]
    top = pick(routing, place, arrived_ups)
    weights = turn(place, own, after(other, top))
    local1, *terms = held_step(middle_body, weights[1], blocks1 + [top], [block] * 5)

    terms = [terms[0]] + [along_x(terms[d], d) for d in (1, 2, 3)]
    keep, give = order(place, [after(blocks0[0], local1)] + blocks0[1:] + blocks1)
    rows = pairs(keep, swap(give))
    rows = [rows[0]] + [along_mine(rows[e], e) for e in (1, 2, 3)]
    cotangent, keep, give, *sends = held_step(
        backward_body, weights[0], terms + [after(top, rows[0]), slope, local1, place], [block] * 7
    )

    ends = [sends[0]] + [along_x(sends[d], d) for d in (1, 2, 3)]
    local = pair(keep, swap(give))
    local = [local] + [along_mine(local, e) for e in (1, 2, 3)]
    grad = pl.pallas_call(
        last_kernel,
        in_specs=[SCALARS, SCALARS] + [WHOLE] * 5,
        out_specs=WHOLE,
        out_shape=block,
        compiler_params=SMALL,
    )(image_counts, place, *ends, after(cotangent, *rows[1:], local[0]))
    grad = pair(grad, swap(grad))
    going = after(grad, local[1], local[3])
    grads = [grad] + [along_mine(going, e) for e in (1, 2, 3)]

    parts = weight_grad(place, [after(rows[0], grad)] + rows[1:], local)
    llm_grad = parts[0].astype(F32)
    for j in (1, 2, 3):
        llm_grad = llm_grad + along_other(parts[j], j).astype(F32)
    llm_grad = llm_grad[None]

    parts = merger_parts(place, [acts[0]] + acts[1:], grads)
    merger_grad = parts[0].astype(F32)
    for j in (1, 2, 3):
        merger_grad = merger_grad + along_other(parts[j], j).astype(F32)
    return (llm_grad, merger_grad)


def solution(mesh):
    return jax.shard_map(
        on_device,
        mesh=mesh,
        in_specs=(
            P(("segment", "dp"), None, None),
            P(None, "mp"),
            P(),
            P(),
            P(None, "dp", "mp"),
            P("segment", None, "mp"),
            P(None, "dp", "mp"),
        ),
        out_specs=(P("segment", "dp", "mp"), P(("segment", "dp"), "mp")),
        check_vma=False,
    )
```
